512 devices in a mesh: row: 16 (over z_lo, x), col: 32 (over z_hi, y, core).
Axes of the slice: x: 4, y: 8, z: 8 (z_hi: 2, z_lo: 4; z = z_hi * 4 + z_lo), core: 2. Of those that a mesh axis runs over, the one named last changes fastest.
Arguments:
- values: float32 [8192, 8192], P('col', 'row'), may hold values from 0.01 to 100, as said below
- pattern: int32 [64, 64], replicated, may hold values from 0 to 1, as said below
- prune: int32 [64, 64], P('col', 'row'), may hold values from 0 to 1, as said below
Outputs:
- clustered: float32 [8192, 8192], P('col', 'row')
The draws below stay inside these ranges and needn't reach their ends.
Inputs may be any that keep to these rules, and one draw needn't show every extreme that they name: `values`: all positive. `pattern`: every diagonal tile is 1. A block is the tiles of rows a * 2 to a * 2 + 1 and columns b * 4 to b * 4 + 3; every block holds at most 2 ones, and for some a every block of block row a, and for some b every block of block column b, holds exactly 2. `prune`: every diagonal tile is 1.
All inputs are finite; a program needn't handle non-finite values.
Results may differ from the reference program's by a relative error of at most 0.0015.
Values may be sent and summed in bfloat16 or wider, within the bound.
A program may use at most 64 MiB of HBM per device.

```python
import math
import jax
import jax.numpy as jnp

TILE = 128
TR_DEV = 2
NT = 64
TC_DEV = 4
MAXB = 2
ORDER = 8192


def draw_values(key, part):
    key = jax.random.fold_in(key, 1)
    first, second, third = jax.random.split(key, 3)
    base = jnp.exp(jax.random.uniform(first, (ORDER, ORDER), jnp.float32, math.log(0.01), 0.0))
    row_scale = jnp.exp(jax.random.uniform(second, (ORDER, 1), jnp.float32, 0.0, math.log(10.0)))
    col_scale = jnp.exp(jax.random.uniform(third, (1, ORDER), jnp.float32, 0.0, math.log(10.0)))
    return base * row_scale * col_scale


def draw_pattern(key, part):
    key = jax.random.fold_in(key, 2)
    first, second, third, fourth = jax.random.split(key, 4)
    block_rows = NT // TR_DEV
    block_cols = NT // TC_DEV
    block_tiles = TR_DEV * TC_DEV
    counts = jnp.maximum(jax.random.randint(first, (block_rows, block_cols), -6, MAXB + 1), 0)
    chosen_row = jax.random.randint(second, (), 0, block_rows)
    chosen_col = jax.random.randint(third, (), 0, block_cols)
    row_ids = jnp.arange(block_rows)[:, None]
    col_ids = jnp.arange(block_cols)[None, :]
    counts = jnp.where((row_ids == chosen_row) | (col_ids == chosen_col), MAXB, counts)
    tile_row = jnp.arange(NT)[:, None]
    tile_col = jnp.arange(NT)[None, :]
    diagonal = tile_row == tile_col
    diag_counts = diagonal.astype(jnp.int32).reshape(block_rows, TR_DEV, block_cols, TC_DEV).sum(axis=(1, 3))
    counts = jnp.maximum(counts, diag_counts)
    ticket = jax.random.randint(fourth, (NT, NT), 0, 4096)
    within = tile_row % TR_DEV * TC_DEV + tile_col % TC_DEV
    scores = jnp.where(diagonal, within, (ticket + 1) * block_tiles + within)
    blocked = scores.reshape(block_rows, TR_DEV, block_cols, TC_DEV).transpose(0, 2, 1, 3).reshape(block_rows, block_cols, block_tiles)
    ranks = jnp.sum((blocked[:, :, None, :] < blocked[:, :, :, None]).astype(jnp.int32), axis=3)
    keeping = (ranks < counts[:, :, None]).astype(jnp.int32)
    return keeping.reshape(block_rows, block_cols, TR_DEV, TC_DEV).transpose(0, 2, 1, 3).reshape(NT, NT)


def draw_prune(key, part):
    key = jax.random.fold_in(key, 3)
    ticket = jax.random.randint(key, (NT, NT), 0, 4)
    kept = (ticket > 0).astype(jnp.int32)
    diag = (jnp.arange(NT)[:, None] == jnp.arange(NT)[None, :]).astype(jnp.int32)
    return jnp.maximum(kept, diag)


def setup_inputs(seed: int = 0) -> dict:
    keys = jax.random.split(jax.random.key(seed), 4)
    values = draw_values(jax.random.fold_in(keys[3], 71), 0)
    pattern = draw_pattern(jax.random.fold_in(keys[3], 71), 0)
    prune = draw_prune(jax.random.fold_in(keys[3], 71), 0)
    return dict(values=values, pattern=pattern, prune=prune)


def expand(mask):
    wide = jnp.repeat(mask.astype(jnp.float32), TILE, axis=0)
    return jnp.repeat(wide, TILE, axis=1)


def reference(values, pattern, prune):
    masked = values * expand(pattern)
    in_total = jnp.sum(masked, axis=0)
    stoch = (masked / in_total[None, :]).astype(jnp.bfloat16)
    square = jnp.dot(stoch, stoch, preferred_element_type=jnp.float32)
    inflated = square * square * expand(prune)
    out_total = jnp.sum(inflated, axis=0)
    return ORDER * inflated / out_total[None, :]
```

```python
import functools

import jax
import jax.numpy as jnp
from jax import lax
from jax.experimental import pallas as pl
from jax.experimental.pallas import tpu as pltpu
from jax.sharding import PartitionSpec as P

TILE = 128
SLOTS = 2
CORES = 2
Z_HI = 2
Z_LO = 4


def kernel(
    rows,
    cols,
    values_hbm,
    pattern,
    prune,
    out_hbm,
    values,
    a_pack,
    b_pack,
    in_own,
    in_parts,
    in_total,
    out_own,
    out_parts,
    result,
    b_slot,
    a_row,
    a_col,
    load_sem,
    store_sem,
    in_send,
    in_recv,
    out_send,
    out_recv,
    a_send,
    a_recv,
    b_send,
    b_recv,
):
    tr, tc = prune.shape
    x_size = rows // Z_LO
    y_size = cols // (CORES * Z_HI)
    r, c = lax.axis_index("row"), lax.axis_index("col")
    zl, x = r // x_size, r % x_size
    core = c % CORES
    y = (c // CORES) % y_size
    zh = c // (CORES * y_size)

    def row_of(zl_, x_):
        return zl_ * x_size + x_

    def col_of(zh_, y_, core_):
        return (zh_ * y_size + y_) * CORES + core_

    loads = [
        pltpu.make_async_copy(
            values_hbm.at[pl.ds(t // tc * TILE, TILE), pl.ds(t % tc * TILE, TILE)],
            values.at[t],
            load_sem.at[t],
        )
        for t in range(tr * tc)
    ]
    for load in loads:
        load.start()

    barrier = pltpu.get_barrier_semaphore()

    def greet_col(d, carry):
        pl.semaphore_signal(barrier, inc=1, device_id={"col": (c + d) % cols})
        return carry

    lax.fori_loop(1, cols, greet_col, 0)
    row_peers = [row_of((zl + d) % Z_LO, x) for d in range(1, Z_LO)]
    row_peers += [row_of(zl, (x + d) % x_size) for d in range(1, x_size)]
    for peer in row_peers:
        pl.semaphore_signal(barrier, inc=1, device_id={"row": peer})

    seen = jnp.int32(0)
    place = [jnp.int32(0)] * SLOTS
    place_col = [jnp.int32(0)] * SLOTS
    for t in range(tr * tc):
        here = pattern[tr * c + t // tc, tc * r + t % tc]
        for s in range(SLOTS):
            hit = (here > 0) & (seen == s)
            place[s] = jnp.where(hit, t, place[s])
            place_col[s] = jnp.where(hit, t % tc, place_col[s])
        seen = seen + here

    for load in loads:
        load.wait()
    tiles = []
    partial = [jnp.zeros((1, TILE), jnp.float32) for _ in range(tc)]
    for s in range(SLOTS):
        tile = jnp.where(seen > s, values[place[s]], 0.0)
        tiles.append(tile)
        total = jnp.sum(tile, axis=0, keepdims=True)
        for j in range(tc):
            partial[j] = partial[j] + jnp.where(place_col[s] == j, total, 0.0)
    in_own[...] = jnp.concatenate(partial, axis=1)

    pl.semaphore_wait(barrier, cols - 1 + len(row_peers))

    def exchange(own_ref, parts_ref, send_sem, recv_sem):
        def send(d, carry):
            pltpu.make_async_remote_copy(
                src_ref=own_ref,
                dst_ref=parts_ref.at[cols - 1 - d],
                send_sem=send_sem,
                recv_sem=recv_sem,
                device_id={"col": (c + d) % cols},
            ).start()
            return carry

        lax.fori_loop(1, cols, send, 0)

    def collect(own_ref, parts_ref, recv_sem):
        pltpu.make_async_copy(parts_ref, parts_ref, recv_sem).wait()
        return own_ref[...] + jnp.sum(parts_ref[...], axis=0)

    def drain(parts_ref, send_sem):
        pltpu.make_async_copy(parts_ref, parts_ref, send_sem).wait()

    exchange(in_own, in_parts, in_send, in_recv)
    in_sum = collect(in_own, in_parts, in_recv)
    for j in range(tc):
        in_total[j] = in_sum[:, j * TILE : (j + 1) * TILE]
    for s in range(SLOTS):
        stoch = (tiles[s] / in_total[place_col[s]]).astype(jnp.bfloat16)
        a_pack[SLOTS * r + s] = stoch
        b_pack[SLOTS * c + s] = stoch
    b_pack[SLOTS * cols] = jnp.zeros((TILE, TILE), jnp.bfloat16)

    a_count, b_count = 0, 0

    def packed(ref, origin):
        return ref.at[pl.ds(SLOTS * origin, SLOTS)]

    def arrived(ref, origin, sem):
        pltpu.make_async_copy(packed(ref, origin), packed(ref, origin), sem).wait()

    def send_a(origin, peer):
        nonlocal a_count
        pltpu.make_async_remote_copy(
            src_ref=packed(a_pack, origin),
            dst_ref=packed(a_pack, origin),
            send_sem=a_send.at[a_count],
            recv_sem=a_recv.at[origin],
            device_id={"row": peer},
        ).start()
        a_count += 1

    def send_b(origin, peer):
        nonlocal b_count
        pltpu.make_async_remote_copy(
            src_ref=packed(b_pack, origin),
            dst_ref=packed(b_pack, origin),
            send_sem=b_send.at[b_count],
            recv_sem=b_recv.at[origin],
            device_id={"col": peer},
        ).start()
        b_count += 1

    def wait_a(origin):
        arrived(a_pack, origin, a_recv.at[origin])

    def wait_b(origin):
        arrived(b_pack, origin, b_recv.at[origin])

    sibling = col_of(zh, y, 1 - core)
    up = col_of(zh, (y + 1) % y_size, core)
    down = col_of(zh, (y + y_size - 1) % y_size, core)
    other = 1 - zh
    half = y_size // 2

    def around_x(origin):
        for d in (1, x_size - 1, *range(2, x_size - 1)):
            send_a(origin, row_of(zl, (x + d) % x_size))

    send_b(c, up)
    send_b(c, down)
    around_x(r)
    send_b(c, col_of(other, y, core))
    for d in range(1, Z_LO):
        send_a(r, row_of((zl + d) % Z_LO, x))
    send_b(c, sibling)

    def locate_b(block, carry):
        count = jnp.int32(0)
        for t in range(tr * tc):
            here = pattern[tr * block + t // tc, tc * r + t % tc]
            b_slot[block * tr * tc + t] = jnp.where(here > 0, SLOTS * block + count, SLOTS * cols)
            count = count + here
        return carry

    lax.fori_loop(0, cols, locate_b, 0)

    def locate_a(block, carry):
        count = jnp.int32(0)
        row_ = [jnp.int32(tr)] * SLOTS
        col_ = [jnp.int32(0)] * SLOTS
        for t in range(tr * tc):
            here = pattern[tr * c + t // tc, tc * block + t % tc]
            for s in range(SLOTS):
                hit = (here > 0) & (count == s)
                row_[s] = jnp.where(hit, t // tc, row_[s])
                col_[s] = jnp.where(hit, t % tc, col_[s])
            count = count + here
        for s in range(SLOTS):
            a_row[block * SLOTS + s] = row_[s]
            a_col[block * SLOTS + s] = tc * (tc * block + col_[s])
        return carry

    lax.fori_loop(0, rows, locate_a, 0)

    def pass_on(origin, peer, last):
        wait_b(origin)
        if not last:
            send_b(origin, peer)
        send_b(origin, sibling)

    for step in range(1, half + 1):
        pass_on(col_of(zh, (y + y_size - step) % y_size, core), up, step == half)
        if step < half:
            pass_on(col_of(zh, (y + step) % y_size, core), down, step == half - 1)
        if step < Z_LO:
            origin = row_of((zl + step) % Z_LO, x)
            wait_a(origin)
            around_x(origin)
        if step == 1:
            origin = col_of(other, y, core)
            wait_b(origin)
            send_b(origin, up)
            send_b(origin, down)
            send_b(origin, sibling)
        else:
            pass_on(col_of(other, (y + y_size - step + 1) % y_size, core), up, step == half)
            pass_on(col_of(other, (y + step - 1) % y_size, core), down, False)
    pass_on(col_of(other, (y + half) % y_size, core), down, True)

    for zl_ in range(Z_LO):
        for d in range(1, x_size):
            wait_a(row_of((zl + zl_) % Z_LO, (x + d) % x_size))

    def wait_sibling(block, carry):
        wait_b(block * CORES + 1 - core)
        return carry

    lax.fori_loop(0, cols // CORES, wait_sibling, 0)

    result[...] = jnp.zeros_like(result)

    def multiply(block, carry):
        left, right = [], []
        for s in range(SLOTS):
            row_ = a_row[block * SLOTS + s]
            k = a_col[block * SLOTS + s]
            tile = a_pack[block * SLOTS + s]
            left.append(
                jnp.concatenate(
                    [jnp.where(row_ == i, tile, jnp.zeros_like(tile)) for i in range(tr)], axis=0
                )
            )
            right.append(jnp.concatenate([b_pack[b_slot[k + j]] for j in range(tc)], axis=1))
        result[...] += jnp.dot(
            jnp.concatenate(left, axis=1),
            jnp.concatenate(right, axis=0),
            preferred_element_type=jnp.float32,
        )
        return carry

    lax.fori_loop(0, rows, multiply, 0)

    sums = []
    for j in range(tc):
        col_sum = jnp.zeros((1, TILE), jnp.float32)
        for i in range(tr):
            at = (slice(i * TILE, (i + 1) * TILE), slice(j * TILE, (j + 1) * TILE))
            square = result[at]
            inflated = jnp.where(prune[i, j] > 0, square * square, 0.0)
            result[at] = inflated
            col_sum = col_sum + jnp.sum(inflated, axis=0, keepdims=True)
        sums.append(col_sum)
    out_own[...] = jnp.concatenate(sums, axis=1)

    exchange(out_own, out_parts, out_send, out_recv)
    drain(in_parts, in_send)
    for n in range(a_count):
        arrived(a_pack, 0, a_send.at[n])
    for n in range(b_count):
        arrived(b_pack, 0, b_send.at[n])
    out_sum = collect(out_own, out_parts, out_recv)
    order = tr * TILE * cols
    result[...] = result[...] * (order / out_sum)
    store = pltpu.make_async_copy(result, out_hbm, store_sem)
    store.start()
    drain(out_parts, out_send)
    store.wait()


def on_device(rows, cols, values, pattern, prune):
    tr, tc = prune.shape
    height, width = values.shape
    f32, bf16 = jnp.float32, jnp.bfloat16
    dma = pltpu.SemaphoreType.DMA
    return pl.pallas_call(
        functools.partial(kernel, rows, cols),
        out_shape=jax.ShapeDtypeStruct((height, width), f32),
        in_specs=[
            pl.BlockSpec(memory_space=pl.ANY),
            pl.BlockSpec(memory_space=pltpu.SMEM),
            pl.BlockSpec(memory_space=pltpu.SMEM),
        ],
        out_specs=pl.BlockSpec(memory_space=pl.ANY),
        scratch_shapes=[
            pltpu.VMEM((tr * tc, TILE, TILE), f32),
            pltpu.VMEM((rows * SLOTS, TILE, TILE), bf16),
            pltpu.VMEM((cols * SLOTS + 1, TILE, TILE), bf16),
            pltpu.VMEM((1, width), f32),
            pltpu.VMEM((cols - 1, 1, width), f32),
            pltpu.VMEM((tc, 1, TILE), f32),
            pltpu.VMEM((1, width), f32),
            pltpu.VMEM((cols - 1, 1, width), f32),
            pltpu.VMEM((height, width), f32),
            pltpu.SMEM((cols * tr * tc,), jnp.int32),
            pltpu.SMEM((rows * SLOTS,), jnp.int32),
            pltpu.SMEM((rows * SLOTS,), jnp.int32),
            dma((tr * tc,)),
            dma,
            dma,
            dma,
            dma,
            dma,
            dma((rows,)),
            dma((rows,)),
            dma((cols,)),
            dma((cols,)),
        ],
        compiler_params=pltpu.CompilerParams(
            collective_id=0,
            has_side_effects=True,
            vmem_limit_bytes=32 * 1024 * 1024,
        ),
        cost_estimate=pl.CostEstimate(
            flops=2 * height * width * TILE * SLOTS * rows,
            bytes_accessed=2 * 4 * height * width,
            transcendentals=0,
        ),
    )(values, pattern, prune)


def solution(mesh):
    in_specs = (P("col", "row"), P(), P("col", "row"))
    out_specs = P("col", "row")
    return jax.shard_map(
        functools.partial(on_device, mesh.shape["row"], mesh.shape["col"]),
        mesh=mesh,
        in_specs=in_specs,
        out_specs=out_specs,
        check_vma=False,
    )
```

```python
import functools

import jax
import jax.numpy as jnp
from jax import lax
from jax.experimental import pallas as pl
from jax.experimental.pallas import tpu as pltpu
from jax.sharding import PartitionSpec as P

TILE = 128
SLOTS = 2
CORES = 2
Z_HI = 2
Z_LO = 4


def kernel(
    rows,
    cols,
    values_hbm,
    pattern_hbm,
    prune_hbm,
    result_hbm,
    scale_hbm,
    values,
    pattern,
    prune,
    raw_own,
    raw_other,
    scale,
    a_pack,
    b_pack,
    in_own,
    in_parts,
    in_total,
    out_own,
    out_parts,
    result,
    b_slot,
    a_row,
    a_col,
    load_sem,
    store_sem,
    fetch_sem,
    raw_sem,
    far_send,
    far_recv,
    in_send,
    in_recv,
    out_send,
    out_recv,
    a_send,
    a_recv,
    b_send,
    b_recv,
):
    tr, tc = prune.shape
    x_size = rows // Z_LO
    y_size = cols // (CORES * Z_HI)
    r, c = lax.axis_index("row"), lax.axis_index("col")
    zl, x = r // x_size, r % x_size
    core = c % CORES
    y = (c // CORES) % y_size
    zh = c // (CORES * y_size)

    def row_of(zl_, x_):
        return zl_ * x_size + x_

    def col_of(zh_, y_, core_):
        return (zh_ * y_size + y_) * CORES + core_

    loads = [
        pltpu.make_async_copy(
            values_hbm.at[pl.ds(t // tc * TILE, TILE), pl.ds(t % tc * TILE, TILE)],
            values.at[t],
            load_sem.at[t],
        )
        for t in range(tr * tc)
    ]
    fetches = [
        pltpu.make_async_copy(pattern_hbm, pattern, fetch_sem.at[0]),
        pltpu.make_async_copy(prune_hbm, prune, fetch_sem.at[1]),
    ]
    for copy in fetches + loads:
        copy.start()

    barrier = pltpu.get_barrier_semaphore()

    def greet_col(d, carry):
        pl.semaphore_signal(barrier, inc=1, device_id={"col": (c + d) % cols})
        return carry

    lax.fori_loop(1, cols, greet_col, 0)
    row_peers = [row_of((zl + d) % Z_LO, x) for d in range(1, Z_LO)]
    row_peers += [row_of(zl, (x + d) % x_size) for d in range(1, x_size)]
    for peer in row_peers:
        pl.semaphore_signal(barrier, inc=1, device_id={"row": peer})

    for copy in fetches:
        copy.wait()

    def locate(block_row, block_col):
        seen = jnp.int32(0)
        place = [jnp.int32(0)] * SLOTS
        place_col = [jnp.int32(0)] * SLOTS
        for t in range(tr * tc):
            here = pattern[tr * block_row + t // tc, tc * block_col + t % tc]
            for s in range(SLOTS):
                hit = (here > 0) & (seen == s)
                place[s] = jnp.where(hit, t, place[s])
                place_col[s] = jnp.where(hit, t % tc, place_col[s])
            seen = seen + here
        return seen, place, place_col

    seen, place, place_col = locate(c, r)
    for copy in loads:
        copy.wait()
    tiles = []
    partial = [jnp.zeros((1, TILE), jnp.float32) for _ in range(tc)]
    for s in range(SLOTS):
        tile = jnp.where(seen > s, values[place[s]], 0.0)
        tiles.append(tile)
        raw_own[s] = tile
        total = jnp.sum(tile, axis=0, keepdims=True)
        for j in range(tc):
            partial[j] = partial[j] + jnp.where(place_col[s] == j, total, 0.0)
    in_own[...] = jnp.concatenate(partial, axis=1)

    pl.semaphore_wait(barrier, cols - 1 + len(row_peers))

    def exchange(own_ref, parts_ref, send_sem, recv_sem):
        def send(d, carry):
            pltpu.make_async_remote_copy(
                src_ref=own_ref,
                dst_ref=parts_ref.at[cols - 1 - d],
                send_sem=send_sem,
                recv_sem=recv_sem,
                device_id={"col": (c + d) % cols},
            ).start()
            return carry

        lax.fori_loop(1, cols, send, 0)

    def collect(own_ref, parts_ref, recv_sem):
        pltpu.make_async_copy(parts_ref, parts_ref, recv_sem).wait()
        return own_ref[...] + jnp.sum(parts_ref[...], axis=0)

    def drain(parts_ref, send_sem):
        pltpu.make_async_copy(parts_ref, parts_ref, send_sem).wait()

    other = 1 - zh
    partner = col_of(other, y, core)
    exchange(in_own, in_parts, in_send, in_recv)
    raw_copy = pltpu.make_async_remote_copy(
        src_ref=raw_own,
        dst_ref=raw_other,
        send_sem=raw_sem.at[0],
        recv_sem=raw_sem.at[1],
        device_id={"col": partner},
    )
    raw_copy.start()

    def locate_b(block, carry):
        count = jnp.int32(0)
        for t in range(tr * tc):
            here = pattern[tr * block + t // tc, tc * r + t % tc]
            b_slot[block * tr * tc + t] = jnp.where(here > 0, SLOTS * block + count, SLOTS * cols)
            count = count + here
        return carry

    lax.fori_loop(0, cols, locate_b, 0)

    def locate_a(block, carry):
        count = jnp.int32(0)
        row_ = [jnp.int32(tr)] * SLOTS
        col_ = [jnp.int32(0)] * SLOTS
        for t in range(tr * tc):
            here = pattern[tr * c + t // tc, tc * block + t % tc]
            for s in range(SLOTS):
                hit = (here > 0) & (count == s)
                row_[s] = jnp.where(hit, t // tc, row_[s])
                col_[s] = jnp.where(hit, t % tc, col_[s])
            count = count + here
        for s in range(SLOTS):
            a_row[block * SLOTS + s] = row_[s]
            a_col[block * SLOTS + s] = tc * (tc * block + col_[s])
        return carry

    lax.fori_loop(0, rows, locate_a, 0)

    _, _, other_col = locate(partner, r)
    in_sum = collect(in_own, in_parts, in_recv)
    for j in range(tc):
        in_total[j] = in_sum[:, j * TILE : (j + 1) * TILE]
    for s in range(SLOTS):
        stoch = (tiles[s] / in_total[place_col[s]]).astype(jnp.bfloat16)
        a_pack[SLOTS * r + s] = stoch
        b_pack[SLOTS * c + s] = stoch
    b_pack[SLOTS * cols] = jnp.zeros((TILE, TILE), jnp.bfloat16)

    a_count, b_count = 0, 0

    def packed(ref, origin):
        return ref.at[pl.ds(SLOTS * origin, SLOTS)]

    def arrived(ref, origin, sem):
        pltpu.make_async_copy(packed(ref, origin), packed(ref, origin), sem).wait()

    def send_a(origin, peer):
        nonlocal a_count
        pltpu.make_async_remote_copy(
            src_ref=packed(a_pack, origin),
            dst_ref=packed(a_pack, origin),
            send_sem=a_send.at[a_count],
            recv_sem=a_recv.at[origin],
            device_id={"row": peer},
        ).start()
        a_count += 1

    def send_b(origin, peer):
        nonlocal b_count
        pltpu.make_async_remote_copy(
            src_ref=packed(b_pack, origin),
            dst_ref=packed(b_pack, origin),
            send_sem=b_send.at[b_count],
            recv_sem=b_recv.at[origin],
            device_id={"col": peer},
        ).start()
        b_count += 1

    def wait_a(origin):
        arrived(a_pack, origin, a_recv.at[origin])

    def wait_b(origin):
        arrived(b_pack, origin, b_recv.at[origin])

    sibling = col_of(zh, y, 1 - core)
    half = y_size // 2

    def y_at(zh_, d):
        return col_of(zh_, (y + d + y_size) % y_size, core)

    def around_x(origin):
        for d in (1, x_size - 1, *range(2, x_size - 1)):
            send_a(origin, row_of(zl, (x + d) % x_size))

    def around_y(origin):
        for d in (1, -1, 2, -2):
            send_b(origin, y_at(zh, d))
        send_b(origin, sibling)

    def send_far(origin, s, sign):
        nonlocal far_count
        tile = b_pack.at[SLOTS * origin + s]
        pltpu.make_async_remote_copy(
            src_ref=tile,
            dst_ref=tile,
            send_sem=far_send.at[far_count],
            recv_sem=far_recv.at[far_count],
            device_id={"col": y_at(zh, sign)},
        ).start()
        far_count += 1

    def near(zh_, d):
        wait_b(y_at(zh_, d))
        send_b(y_at(zh_, d), sibling)

    def forward(zh_, d):
        wait_b(y_at(zh_, d))
        send_b(y_at(zh_, d), y_at(zh, -1 if d > 0 else 1))
        send_b(y_at(zh_, d), sibling)

    def forward_far(zh_, d):
        wait_b(y_at(zh_, d))
        send_far(y_at(zh_, d), 0 if d > 0 else 1, -1 if d > 0 else 1)
        send_b(y_at(zh_, d), sibling)

    def z_arrival(d):
        origin = row_of((zl + d) % Z_LO, x)
        wait_a(origin)
        around_x(origin)

    far_count = 0
    around_y(c)
    for d in (1, 3, 2):
        send_a(r, row_of((zl + d) % Z_LO, x))
    around_x(r)
    raw_copy.wait_recv()
    for s in range(SLOTS):
        stoch = (raw_other[s] / in_total[other_col[s]]).astype(jnp.bfloat16)
        b_pack[SLOTS * partner + s] = stoch
    around_y(partner)

    near(zh, 1)
    near(zh, -1)
    z_arrival(1)
    z_arrival(3)
    forward(zh, 2)
    forward(zh, -2)
    z_arrival(2)
    near(other, 1)
    near(other, -1)
    forward(other, 2)
    forward(other, -2)
    forward_far(zh, 3)
    forward_far(zh, -3)
    forward_far(other, 3)
    forward_far(other, -3)
    for n, zh_ in ((0, zh), (2, other)):
        origin = y_at(zh_, half)
        for s in range(SLOTS):
            tile = b_pack.at[SLOTS * origin + s]
            pltpu.make_async_copy(tile, tile, far_recv.at[n + s]).wait()
        send_b(origin, sibling)

    for zl_ in range(Z_LO):
        for d in range(1, x_size):
            wait_a(row_of((zl + zl_) % Z_LO, (x + d) % x_size))

    def wait_sibling(block, carry):
        wait_b(block * CORES + 1 - core)
        return carry

    lax.fori_loop(0, cols // CORES, wait_sibling, 0)

    result[...] = jnp.zeros_like(result)

    def multiply(block, carry):
        left, right = [], []
        for s in range(SLOTS):
            row_ = a_row[block * SLOTS + s]
            k = a_col[block * SLOTS + s]
            tile = a_pack[block * SLOTS + s]
            left.append(
                jnp.concatenate(
                    [jnp.where(row_ == i, tile, jnp.zeros_like(tile)) for i in range(tr)], axis=0
                )
            )
            right.append(jnp.concatenate([b_pack[b_slot[k + j]] for j in range(tc)], axis=1))
        result[...] += jnp.dot(
            jnp.concatenate(left, axis=1),
            jnp.concatenate(right, axis=0),
            preferred_element_type=jnp.float32,
        )
        return carry

    lax.fori_loop(0, rows, multiply, 0, unroll=4)

    sums = []
    for j in range(tc):
        col_sum = jnp.zeros((1, TILE), jnp.float32)
        for i in range(tr):
            at = (slice(i * TILE, (i + 1) * TILE), slice(j * TILE, (j + 1) * TILE))
            square = result[at]
            inflated = jnp.where(prune[i, j] > 0, square * square, 0.0)
            result[at] = inflated
            col_sum = col_sum + jnp.sum(inflated, axis=0, keepdims=True)
        sums.append(col_sum)
    out_own[...] = jnp.concatenate(sums, axis=1)

    exchange(out_own, out_parts, out_send, out_recv)
    store = pltpu.make_async_copy(result, result_hbm, store_sem.at[0])
    store.start()
    raw_copy.wait_send()
    drain(in_parts, in_send)
    for n in range(a_count):
        arrived(a_pack, 0, a_send.at[n])
    for n in range(b_count):
        arrived(b_pack, 0, b_send.at[n])
    for n in range(far_count):
        pltpu.make_async_copy(b_pack.at[0], b_pack.at[0], far_send.at[n]).wait()
    out_sum = collect(out_own, out_parts, out_recv)
    order = tr * TILE * cols
    scale[...] = order / out_sum
    store_scale = pltpu.make_async_copy(scale, scale_hbm, store_sem.at[1])
    store_scale.start()
    drain(out_parts, out_send)
    store.wait()
    store_scale.wait()


def on_device(rows, cols, values, pattern, prune):
    tr, tc = prune.shape
    height, width = values.shape
    f32, bf16 = jnp.float32, jnp.bfloat16
    dma = pltpu.SemaphoreType.DMA
    inflated, scale = pl.pallas_call(
        functools.partial(kernel, rows, cols),
        out_shape=[
            jax.ShapeDtypeStruct((height, width), f32),
            jax.ShapeDtypeStruct((1, width), f32),
        ],
        in_specs=[pl.BlockSpec(memory_space=pl.ANY)] * 3,
        out_specs=[pl.BlockSpec(memory_space=pl.ANY)] * 2,
        scratch_shapes=[
            pltpu.VMEM((tr * tc, TILE, TILE), f32),
            pltpu.SMEM(pattern.shape, jnp.int32),
            pltpu.SMEM(prune.shape, jnp.int32),
            pltpu.VMEM((SLOTS, TILE, TILE), f32),
            pltpu.VMEM((SLOTS, TILE, TILE), f32),
            pltpu.VMEM((1, width), f32),
            pltpu.VMEM((rows * SLOTS, TILE, TILE), bf16),
            pltpu.VMEM((cols * SLOTS + 1, TILE, TILE), bf16),
            pltpu.VMEM((1, width), f32),
            pltpu.VMEM((cols - 1, 1, width), f32),
            pltpu.VMEM((tc, 1, TILE), f32),
            pltpu.VMEM((1, width), f32),
            pltpu.VMEM((cols - 1, 1, width), f32),
            pltpu.VMEM((height, width), f32),
            pltpu.SMEM((cols * tr * tc,), jnp.int32),
            pltpu.SMEM((rows * SLOTS,), jnp.int32),
            pltpu.SMEM((rows * SLOTS,), jnp.int32),
            dma((tr * tc,)),
            dma((2,)),
            dma((2,)),
            dma((2,)),
            dma((4,)),
            dma((4,)),
            dma,
            dma,
            dma,
            dma,
            dma((rows,)),
            dma((rows,)),
            dma((cols,)),
            dma((cols,)),
        ],
        compiler_params=pltpu.CompilerParams(
            collective_id=0,
            has_side_effects=True,
            vmem_limit_bytes=60 * 1024 * 1024,
        ),
        cost_estimate=pl.CostEstimate(
            flops=2 * height * width * TILE * SLOTS * rows,
            bytes_accessed=2 * 4 * height * width,
            transcendentals=0,
        ),
    )(values, pattern, prune)
    return inflated * scale


def solution(mesh):
    in_specs = (P("col", "row"), P(), P("col", "row"))
    out_specs = P("col", "row")
    return jax.shard_map(
        functools.partial(on_device, mesh.shape["row"], mesh.shape["col"]),
        mesh=mesh,
        in_specs=in_specs,
        out_specs=out_specs,
        check_vma=False,
    )
```

```python
import functools

import jax
import jax.numpy as jnp
from jax import lax
from jax.experimental import pallas as pl
from jax.experimental.pallas import tpu as pltpu
from jax.sharding import PartitionSpec as P

TILE = 128
SLOTS = 2
CORES = 2
Z_HI = 2
Z_LO = 4


def kernel(
    rows,
    cols,
    values_hbm,
    pattern_hbm,
    prune_hbm,
    result_hbm,
    scale_hbm,
    values,
    pattern,
    prune,
    raw_own,
    raw_in,
    pair_part,
    in_pair,
    scale,
    a_pack,
    b_pack,
    in_own,
    in_parts,
    in_total,
    out_own,
    out_parts,
    result,
    b_slot,
    a_row,
    a_col,
    load_sem,
    store_sem,
    fetch_sem,
    raw_send,
    raw_recv,
    pair_sem,
    far_send,
    far_recv,
    in_send,
    in_recv,
    out_send,
    out_recv,
    a_send,
    a_recv,
    b_send,
    b_recv,
):
    tr, tc = prune.shape
    x_size = rows // Z_LO
    y_size = cols // (CORES * Z_HI)
    r, c = lax.axis_index("row"), lax.axis_index("col")
    zl, x = r // x_size, r % x_size
    core = c % CORES
    y = (c // CORES) % y_size
    zh = c // (CORES * y_size)

    def row_of(zl_, x_):
        return zl_ * x_size + x_

    def col_of(zh_, y_, core_):
        return (zh_ * y_size + y_) * CORES + core_

    loads = [
        pltpu.make_async_copy(
            values_hbm.at[pl.ds(t // tc * TILE, TILE), pl.ds(t % tc * TILE, TILE)],
            values.at[t],
            load_sem.at[t],
        )
        for t in range(tr * tc)
    ]
    fetches = [
        pltpu.make_async_copy(pattern_hbm, pattern, fetch_sem.at[0]),
        pltpu.make_async_copy(prune_hbm, prune, fetch_sem.at[1]),
    ]
    for copy in fetches + loads:
        copy.start()

    barrier = pltpu.get_barrier_semaphore()

    other = 1 - zh
    partner = col_of(other, y, core)

    def y_at(zh_, d):
        return col_of(zh_, (y + d + y_size) % y_size, core)

    def ring(d):
        return min(d, y_size - d)

    offsets = [(dz, dy, dc) for dz in range(Z_HI) for dy in range(y_size) for dc in range(CORES)]
    offsets.sort(key=lambda o: -(Z_LO * o[0] + ring(o[1])))
    offsets.remove((0, 0, 0))

    def at_offset(dz, dy, dc):
        return col_of((zh + dz) % Z_HI, (y + dy) % y_size, (core + dc) % CORES)

    all_peers = [at_offset(*o) for o in offsets]
    half_peers = [at_offset(*o) for o in offsets if o[0] == 0]
    row_peers = [row_of((zl + d) % Z_LO, x) for d in range(1, Z_LO)]
    row_peers += [row_of(zl, (x + d) % x_size) for d in range(1, x_size)]
    for peer in [partner, *half_peers]:
        pl.semaphore_signal(barrier, inc=1, device_id={"col": peer})
    for peer in row_peers:
        pl.semaphore_signal(barrier, inc=1, device_id={"row": peer})
    for copy in fetches:
        copy.wait()

    def locate(block_row, block_col):
        seen = jnp.int32(0)
        place = [jnp.int32(0)] * SLOTS
        place_col = [jnp.int32(0)] * SLOTS
        for t in range(tr * tc):
            here = pattern[tr * block_row + t // tc, tc * block_col + t % tc]
            for s in range(SLOTS):
                hit = (here > 0) & (seen == s)
                place[s] = jnp.where(hit, t, place[s])
                place_col[s] = jnp.where(hit, t % tc, place_col[s])
            seen = seen + here
        return seen, place, place_col

    seen, place, place_col = locate(c, r)
    for copy in loads:
        copy.wait()
    tiles = []
    partial = [jnp.zeros((1, TILE), jnp.float32) for _ in range(tc)]
    for s in range(SLOTS):
        tile = jnp.where(seen > s, values[place[s]], 0.0)
        tiles.append(tile)
        raw_own[s] = tile
        total = jnp.sum(tile, axis=0, keepdims=True)
        for j in range(tc):
            partial[j] = partial[j] + jnp.where(place_col[s] == j, total, 0.0)
    in_own[...] = jnp.concatenate(partial, axis=1)

    pl.semaphore_wait(barrier, 1 + len(half_peers) + len(row_peers))

    def exchange(peers, own_ref, parts_ref, send_sem, recv_sem):
        for n, peer in enumerate(peers):
            pltpu.make_async_remote_copy(
                src_ref=own_ref,
                dst_ref=parts_ref.at[n],
                send_sem=send_sem,
                recv_sem=recv_sem,
                device_id={"col": peer},
            ).start()

    def collect(own_ref, parts_ref, recv_sem):
        pltpu.make_async_copy(parts_ref, parts_ref, recv_sem).wait()
        return own_ref[...] + jnp.sum(parts_ref[...], axis=0)

    def drain(parts_ref, send_sem):
        pltpu.make_async_copy(parts_ref, parts_ref, send_sem).wait()

    exchange([partner], in_own, pair_part, pair_sem.at[0], pair_sem.at[1])
    reach = (2, -2, 1, -1)
    raw_reach = (2, -2)
    raw_sends = []

    def send_raw(peer, slot):
        copy = pltpu.make_async_remote_copy(
            src_ref=raw_own,
            dst_ref=raw_in.at[slot],
            send_sem=raw_send.at[slot],
            recv_sem=raw_recv.at[slot],
            device_id={"col": peer},
        )
        copy.start()
        raw_sends.append(copy)

    send_raw(partner, 0)
    in_pair[...] = collect(in_own, pair_part, pair_sem.at[1])
    exchange(half_peers, in_pair, in_parts, in_send, in_recv)
    for d in raw_reach:
        send_raw(y_at(zh, d), 1 + reach.index(-d))

    def locate_b(block, carry):
        count = jnp.int32(0)
        for t in range(tr * tc):
            here = pattern[tr * block + t // tc, tc * r + t % tc]
            b_slot[block * tr * tc + t] = jnp.where(here > 0, SLOTS * block + count, SLOTS * cols)
            count = count + here
        return carry

    lax.fori_loop(0, cols, locate_b, 0)

    def locate_a(block, carry):
        count = jnp.int32(0)
        row_ = [jnp.int32(tr)] * SLOTS
        col_ = [jnp.int32(0)] * SLOTS
        for t in range(tr * tc):
            here = pattern[tr * c + t // tc, tc * block + t % tc]
            for s in range(SLOTS):
                hit = (here > 0) & (count == s)
                row_[s] = jnp.where(hit, t // tc, row_[s])
                col_[s] = jnp.where(hit, t % tc, col_[s])
            count = count + here
        for s in range(SLOTS):
            a_row[block * SLOTS + s] = row_[s]
            a_col[block * SLOTS + s] = tc * (tc * block + col_[s])
        return carry

    lax.fori_loop(0, rows, locate_a, 0)

    raw_origins = [partner, *(y_at(zh, d) for d in reach)]
    raw_cols = [locate(origin, r)[2] for origin in raw_origins]
    in_sum = collect(in_pair, in_parts, in_recv)
    for j in range(tc):
        in_total[j] = in_sum[:, j * TILE : (j + 1) * TILE]
    for s in range(SLOTS):
        stoch = (tiles[s] / in_total[place_col[s]]).astype(jnp.bfloat16)
        a_pack[SLOTS * r + s] = stoch
        b_pack[SLOTS * c + s] = stoch
    b_pack[SLOTS * cols] = jnp.zeros((TILE, TILE), jnp.bfloat16)

    a_count, b_count = 0, 0

    def packed(ref, origin):
        return ref.at[pl.ds(SLOTS * origin, SLOTS)]

    def arrived(ref, origin, sem):
        pltpu.make_async_copy(packed(ref, origin), packed(ref, origin), sem).wait()

    def send_a(origin, s, peer):
        nonlocal a_count
        pltpu.make_async_remote_copy(
            src_ref=a_pack.at[SLOTS * origin + s],
            dst_ref=a_pack.at[SLOTS * origin + s],
            send_sem=a_send.at[a_count],
            recv_sem=a_recv.at[SLOTS * origin + s],
            device_id={"row": peer},
        ).start()
        a_count += 1

    def send_b(origin, peer):
        nonlocal b_count
        pltpu.make_async_remote_copy(
            src_ref=packed(b_pack, origin),
            dst_ref=packed(b_pack, origin),
            send_sem=b_send.at[b_count],
            recv_sem=b_recv.at[origin],
            device_id={"col": peer},
        ).start()
        b_count += 1

    def wait_a(origin, s):
        tile = a_pack.at[SLOTS * origin + s]
        pltpu.make_async_copy(tile, tile, a_recv.at[SLOTS * origin + s]).wait()

    def wait_b(origin):
        arrived(b_pack, origin, b_recv.at[origin])

    sibling = col_of(zh, y, 1 - core)
    half = y_size // 2

    def around_x(origin, s):
        for d in (*range(2, x_size - 1), 1, x_size - 1):
            send_a(origin, s, row_of(zl, (x + d) % x_size))

    far_count = 0

    def send_far(origin, s, d):
        nonlocal far_count
        tile = b_pack.at[SLOTS * origin + s]
        pltpu.make_async_remote_copy(
            src_ref=tile,
            dst_ref=tile,
            send_sem=far_send.at[far_count],
            recv_sem=far_recv.at[far_count],
            device_id={"col": y_at(zh, d)},
        ).start()
        far_count += 1

    def raw_arrival(n):
        origin = raw_origins[n]
        pltpu.make_async_copy(raw_in.at[n], raw_in.at[n], raw_recv.at[n]).wait()
        for s in range(SLOTS):
            stoch = (raw_in[n, s] / in_total[raw_cols[n][s]]).astype(jnp.bfloat16)
            b_pack[SLOTS * origin + s] = stoch

    def spread(zh_, d):
        sign = -1 if d > 0 else 1
        send_far(y_at(zh_, d), 0 if d > 0 else 1, 2 * sign)
        send_b(y_at(zh_, d), y_at(zh, sign))
        send_b(y_at(zh_, d), sibling)

    def arrive(zh_, d):
        wait_b(y_at(zh_, d))
        send_b(y_at(zh_, d), sibling)

    def z_arrival(d, s):
        origin = row_of((zl + d) % Z_LO, x)
        wait_a(origin, s)
        around_x(origin, s)

    for d in reach:
        if d not in raw_reach:
            send_b(c, y_at(zh, d))
    for s in range(SLOTS):
        for d in (2, 1, 3):
            send_a(r, s, row_of((zl + d) % Z_LO, x))
    for s in range(SLOTS):
        around_x(r, s)
    send_b(c, sibling)
    raw_arrival(0)
    for d in reach:
        send_b(partner, y_at(zh, d))
    send_b(partner, sibling)
    for n, d in enumerate(reach, 1):
        if d in raw_reach:
            raw_arrival(n)
            if abs(d) == 2:
                spread(zh, d)
            else:
                send_b(raw_origins[n], sibling)
    for s in range(SLOTS):
        for d in (1, 3, 2):
            z_arrival(d, s)
    for zh_ in (zh, other):
        for d in reach:
            if zh_ is zh and d in raw_reach:
                continue
            wait_b(y_at(zh_, d))
            if abs(d) == 2:
                spread(zh_, d)
            else:
                send_b(y_at(zh_, d), sibling)
    for zh_, d in ((zh, 3), (zh, -3), (other, 3), (other, -3)):
        arrive(zh_, d)
    for n, zh_ in ((0, zh), (2, other)):
        origin = y_at(zh_, half)
        for s in range(SLOTS):
            tile = b_pack.at[SLOTS * origin + s]
            pltpu.make_async_copy(tile, tile, far_recv.at[n + s]).wait()
        send_b(origin, sibling)

    for zl_ in range(Z_LO):
        for d in range(1, x_size):
            for s in range(SLOTS):
                wait_a(row_of((zl + zl_) % Z_LO, (x + d) % x_size), s)

    def wait_sibling(block, carry):
        wait_b(block * CORES + 1 - core)
        return carry

    lax.fori_loop(0, cols // CORES, wait_sibling, 0)

    result[...] = jnp.zeros_like(result)

    def multiply(block, carry):
        left, right = [], []
        for s in range(SLOTS):
            row_ = a_row[block * SLOTS + s]
            k = a_col[block * SLOTS + s]
            tile = a_pack[block * SLOTS + s]
            left.append(
                jnp.concatenate(
                    [jnp.where(row_ == i, tile, jnp.zeros_like(tile)) for i in range(tr)], axis=0
                )
            )
            right.append(jnp.concatenate([b_pack[b_slot[k + j]] for j in range(tc)], axis=1))
        result[...] += jnp.dot(
            jnp.concatenate(left, axis=1),
            jnp.concatenate(right, axis=0),
            preferred_element_type=jnp.float32,
        )
        return carry

    lax.fori_loop(0, rows, multiply, 0, unroll=4)

    sums = []
    for j in range(tc):
        col_sum = jnp.zeros((1, TILE), jnp.float32)
        for i in range(tr):
            at = (slice(i * TILE, (i + 1) * TILE), slice(j * TILE, (j + 1) * TILE))
            square = result[at]
            inflated = jnp.where(prune[i, j] > 0, square * square, 0.0)
            result[at] = inflated
            col_sum = col_sum + jnp.sum(inflated, axis=0, keepdims=True)
        sums.append(col_sum)
    out_own[...] = jnp.concatenate(sums, axis=1)

    exchange(all_peers, out_own, out_parts, out_send, out_recv)
    store = pltpu.make_async_copy(result, result_hbm, store_sem.at[0])
    store.start()
    drain(pair_part, pair_sem.at[0])
    for copy in raw_sends:
        copy.wait_send()
    drain(in_parts, in_send)
    for n in range(a_count):
        pltpu.make_async_copy(a_pack.at[0], a_pack.at[0], a_send.at[n]).wait()
    for n in range(b_count):
        arrived(b_pack, 0, b_send.at[n])
    for n in range(far_count):
        pltpu.make_async_copy(b_pack.at[0], b_pack.at[0], far_send.at[n]).wait()
    out_sum = collect(out_own, out_parts, out_recv)
    order = tr * TILE * cols
    scale[...] = order / out_sum
    store_scale = pltpu.make_async_copy(scale, scale_hbm, store_sem.at[1])
    store_scale.start()
    drain(out_parts, out_send)
    store.wait()
    store_scale.wait()


def on_device(rows, cols, values, pattern, prune):
    tr, tc = prune.shape
    height, width = values.shape
    f32, bf16 = jnp.float32, jnp.bfloat16
    dma = pltpu.SemaphoreType.DMA
    inflated, scale = pl.pallas_call(
        functools.partial(kernel, rows, cols),
        out_shape=[
            jax.ShapeDtypeStruct((height, width), f32),
            jax.ShapeDtypeStruct((1, width), f32),
        ],
        in_specs=[pl.BlockSpec(memory_space=pltpu.HBM)] * 3,
        out_specs=[pl.BlockSpec(memory_space=pl.ANY)] * 2,
        scratch_shapes=[
            pltpu.VMEM((tr * tc, TILE, TILE), f32),
            pltpu.SMEM(pattern.shape, jnp.int32),
            pltpu.SMEM(prune.shape, jnp.int32),
            pltpu.VMEM((SLOTS, TILE, TILE), f32),
            pltpu.VMEM((5, SLOTS, TILE, TILE), f32),
            pltpu.VMEM((1, 1, width), f32),
            pltpu.VMEM((1, width), f32),
            pltpu.VMEM((1, width), f32),
            pltpu.VMEM((rows * SLOTS, TILE, TILE), bf16),
            pltpu.VMEM((cols * SLOTS + 1, TILE, TILE), bf16),
            pltpu.VMEM((1, width), f32),
            pltpu.VMEM((cols // Z_HI - 1, 1, width), f32),
            pltpu.VMEM((tc, 1, TILE), f32),
            pltpu.VMEM((1, width), f32),
            pltpu.VMEM((cols - 1, 1, width), f32),
            pltpu.VMEM((height, width), f32),
            pltpu.SMEM((cols * tr * tc,), jnp.int32),
            pltpu.SMEM((rows * SLOTS,), jnp.int32),
            pltpu.SMEM((rows * SLOTS,), jnp.int32),
            dma((tr * tc,)),
            dma((2,)),
            dma((2,)),
            dma((5,)),
            dma((5,)),
            dma((2,)),
            dma((4,)),
            dma((4,)),
            dma,
            dma,
            dma,
            dma,
            dma((rows * SLOTS,)),
            dma((rows * SLOTS,)),
            dma((cols,)),
            dma((cols,)),
        ],
        compiler_params=pltpu.CompilerParams(
            collective_id=0,
            has_side_effects=True,
            vmem_limit_bytes=32 * 1024 * 1024,
        ),
        cost_estimate=pl.CostEstimate(
            flops=2 * height * width * TILE * SLOTS * rows,
            bytes_accessed=2 * 4 * height * width,
            transcendentals=0,
        ),
    )(*(pltpu.with_memory_space_constraint(x, pltpu.HBM) for x in (values, pattern, prune)))
    return inflated * scale


def solution(mesh):
    in_specs = (P("col", "row"), P(), P("col", "row"))
    out_specs = P("col", "row")
    return jax.shard_map(
        functools.partial(on_device, mesh.shape["row"], mesh.shape["col"]),
        mesh=mesh,
        in_specs=in_specs,
        out_specs=out_specs,
        check_vma=False,
    )
```

```python
import functools

import jax
import jax.numpy as jnp
from jax import lax
from jax.experimental import pallas as pl
from jax.experimental.pallas import tpu as pltpu
from jax.sharding import PartitionSpec as P

TILE = 128
SLOTS = 2
CORES = 2
Z_HI = 2
Z_LO = 4


def kernel(
    rows,
    cols,
    values_hbm,
    pattern_hbm,
    prune_hbm,
    result_hbm,
    scale_hbm,
    values,
    pattern,
    prune,
    raw_own,
    raw_in,
    pair_part,
    cross_parts,
    in_pair,
    scale,
    a_pack,
    b_pack,
    in_own,
    in_parts,
    in_total,
    out_own,
    out_parts,
    result,
    b_slot,
    a_row,
    a_col,
    load_sem,
    store_sem,
    fetch_sem,
    raw_send,
    raw_recv,
    pair_sem,
    cross_send,
    cross_recv,
    partner_here,
    half_here,
    row_here,
    far_send,
    far_recv,
    in_send,
    in_recv,
    out_send,
    out_recv,
    a_send,
    a_recv,
    b_send,
    b_recv,
):
    tr, tc = prune.shape
    x_size = rows // Z_LO
    y_size = cols // (CORES * Z_HI)
    r, c = lax.axis_index("row"), lax.axis_index("col")
    zl, x = r // x_size, r % x_size
    core = c % CORES
    y = (c // CORES) % y_size
    zh = c // (CORES * y_size)

    def row_of(zl_, x_):
        return zl_ * x_size + x_

    def col_of(zh_, y_, core_):
        return (zh_ * y_size + y_) * CORES + core_

    other = 1 - zh
    partner = col_of(other, y, core)

    def y_at(zh_, d):
        return col_of(zh_, (y + d + y_size) % y_size, core)

    def ring(d):
        return min(d, y_size - d)

    offsets = [(dz, dy, dc) for dz in range(Z_HI) for dy in range(y_size) for dc in range(CORES)]
    offsets.sort(key=lambda o: -(Z_LO * o[0] + ring(o[1])))
    offsets.remove((0, 0, 0))

    def at_offset(dz, dy, dc):
        return col_of((zh + dz) % Z_HI, (y + dy) % y_size, (core + dc) % CORES)

    all_peers = [at_offset(*o) for o in offsets]
    half_peers = [at_offset(*o) for o in offsets if o[0] == 0]
    other_half = [at_offset(*o) for o in offsets if o[0] == 1]

    late_first = (rows - 1 - r) // (rows - 1) * (1 - zh)

    def rank_of(y_, core_):
        side = (y_ + y_size // 2 - 1) // y_size
        first = (y_size - 1 - y_) // (y_size - 1)
        place = ((1 - side) * (2 * y_ - 1) + side * 2 * (y_size - y_) + first) * CORES + core_
        return (place - late_first + cols // Z_HI) % (cols // Z_HI)

    rank = rank_of(y, core)
    half_ranks = [rank_of((y + dy) % y_size, (core + dc) % CORES) for dz, dy, dc in offsets if dz == 0]
    row_peers = [row_of((zl + d) % Z_LO, x) for d in (3, 2, 1)]
    row_peers += [row_of(zl, (x + d) % x_size) for d in range(1, x_size)]
    barrier = pltpu.get_barrier_semaphore()

    def await_some(sem, count):
        pl.when(count > 0)(lambda: pl.semaphore_wait(sem, count))

    def signal(sem, axis, peer):
        pl.semaphore_signal(sem, inc=1, device_id={axis: peer})

    @pl.when(zh == 0)
    def _():
        for peer in other_half:
            signal(barrier, "col", peer)

    for peer, peer_rank in zip(half_peers, half_ranks, strict=True):
        pl.when(peer_rank > rank)(functools.partial(signal, barrier, "col", peer))
    for peer in row_peers:
        pl.when(peer > r)(functools.partial(signal, barrier, "row", peer))
    await_some(barrier, rank + zl + x + zh * (cols // Z_HI))

    @pl.when(zh == 1)
    def _():
        signal(partner_here, "col", partner)

    for peer, peer_rank in zip(half_peers, half_ranks, strict=True):
        pl.when(peer_rank < rank)(functools.partial(signal, half_here, "col", peer))
    for peer in row_peers:
        pl.when(peer < r)(functools.partial(signal, row_here, "row", peer))

    loads = [
        pltpu.make_async_copy(
            values_hbm.at[pl.ds(t // tc * TILE, TILE), pl.ds(t % tc * TILE, TILE)],
            values.at[t],
            load_sem.at[t],
        )
        for t in range(tr * tc)
    ]
    fetches = [
        pltpu.make_async_copy(pattern_hbm, pattern, fetch_sem.at[0]),
        pltpu.make_async_copy(prune_hbm, prune, fetch_sem.at[1]),
    ]
    for copy in fetches + loads:
        copy.start()

    for copy in fetches:
        copy.wait()

    def locate(block_row, block_col):
        seen = jnp.int32(0)
        place = [jnp.int32(0)] * SLOTS
        place_col = [jnp.int32(0)] * SLOTS
        for t in range(tr * tc):
            here = pattern[tr * block_row + t // tc, tc * block_col + t % tc]
            for s in range(SLOTS):
                hit = (here > 0) & (seen == s)
                place[s] = jnp.where(hit, t, place[s])
                place_col[s] = jnp.where(hit, t % tc, place_col[s])
            seen = seen + here
        return seen, place, place_col

    seen, place, place_col = locate(c, r)
    for copy in loads:
        copy.wait()
    tiles = []
    partial = [jnp.zeros((1, TILE), jnp.float32) for _ in range(tc)]
    for s in range(SLOTS):
        tile = jnp.where(seen > s, values[place[s]], 0.0)
        tiles.append(tile)
        raw_own[s] = tile
        total = jnp.sum(tile, axis=0, keepdims=True)
        for j in range(tc):
            partial[j] = partial[j] + jnp.where(place_col[s] == j, total, 0.0)
    in_own[...] = jnp.concatenate(partial, axis=1)

    def exchange(peers, own_ref, parts_ref, send_sem, recv_sem):
        for n, peer in enumerate(peers):
            pltpu.make_async_remote_copy(
                src_ref=own_ref,
                dst_ref=parts_ref.at[n],
                send_sem=send_sem,
                recv_sem=recv_sem,
                device_id={"col": peer},
            ).start()

    def collect(own_ref, parts_ref, recv_sem):
        pltpu.make_async_copy(parts_ref, parts_ref, recv_sem).wait()
        return own_ref[...] + jnp.sum(parts_ref[...], axis=0)

    def drain(parts_ref, send_sem):
        pltpu.make_async_copy(parts_ref, parts_ref, send_sem).wait()

    reach = (2, -2, 1, -1)
    raw_reach = (2, -2)
    raw_origins = [partner, *(y_at(zh, d) for d in raw_reach)]

    def raw_copy(peer, slot):
        return pltpu.make_async_remote_copy(
            src_ref=raw_own,
            dst_ref=raw_in.at[slot],
            send_sem=raw_send.at[slot],
            recv_sem=raw_recv.at[slot],
            device_id={"col": peer},
        )

    raw_sends = [raw_copy(partner, 0)]
    raw_sends += [raw_copy(y_at(zh, d), 1 + raw_reach.index(-d)) for d in raw_reach]

    @pl.when(zh == 1)
    def _():
        exchange(other_half, in_own, cross_parts, cross_send, cross_recv)
        raw_sends[0].start()

    await_some(half_here, cols // Z_HI - 1 - rank)
    exchange(half_peers, in_own, in_parts, in_send, in_recv)
    for copy in raw_sends[1:]:
        copy.start()

    def locate_b(block, carry):
        count = jnp.int32(0)
        for t in range(tr * tc):
            here = pattern[tr * block + t // tc, tc * r + t % tc]
            b_slot[block * tr * tc + t] = jnp.where(here > 0, SLOTS * block + count, SLOTS * cols)
            count = count + here
        return carry

    def locate_a(block, carry):
        count = jnp.int32(0)
        row_ = [jnp.int32(tr)] * SLOTS
        col_ = [jnp.int32(0)] * SLOTS
        for t in range(tr * tc):
            here = pattern[tr * c + t // tc, tc * block + t % tc]
            for s in range(SLOTS):
                hit = (here > 0) & (count == s)
                row_[s] = jnp.where(hit, t // tc, row_[s])
                col_[s] = jnp.where(hit, t % tc, col_[s])
            count = count + here
        for s in range(SLOTS):
            a_row[block * SLOTS + s] = row_[s]
            a_col[block * SLOTS + s] = tc * (tc * block + col_[s])
        return carry

    def locate_all():
        lax.fori_loop(0, cols, locate_b, 0)
        lax.fori_loop(0, rows, locate_a, 0)

    raw_cols = [locate(origin, r)[2] for origin in raw_origins]
    pl.when(zh == 1)(locate_all)
    in_pair[...] = collect(in_own, in_parts, in_recv)

    @pl.when(zh == 0)
    def _():
        pl.semaphore_wait(partner_here, 1)
        exchange([partner], in_pair, pair_part, pair_sem.at[0], pair_sem.at[1])
        raw_sends[0].start()

    def set_total(total):
        for j in range(tc):
            in_total[j] = total[:, j * TILE : (j + 1) * TILE]

    @pl.when(zh == 0)
    def _():
        locate_all()
        set_total(collect(in_pair, cross_parts, cross_recv))

    @pl.when(zh == 1)
    def _():
        set_total(collect(in_pair, pair_part, pair_sem.at[1]))

    for s in range(SLOTS):
        stoch = (tiles[s] / in_total[place_col[s]]).astype(jnp.bfloat16)
        a_pack[SLOTS * r + s] = stoch
        b_pack[SLOTS * c + s] = stoch
    b_pack[SLOTS * cols] = jnp.zeros((TILE, TILE), jnp.bfloat16)

    a_count, b_count = 0, 0

    def packed(ref, origin):
        return ref.at[pl.ds(SLOTS * origin, SLOTS)]

    def arrived(ref, origin, sem):
        pltpu.make_async_copy(packed(ref, origin), packed(ref, origin), sem).wait()

    def send_a(origin, s, peer):
        nonlocal a_count
        pltpu.make_async_remote_copy(
            src_ref=a_pack.at[SLOTS * origin + s],
            dst_ref=a_pack.at[SLOTS * origin + s],
            send_sem=a_send.at[a_count],
            recv_sem=a_recv.at[SLOTS * origin + s],
            device_id={"row": peer},
        ).start()
        a_count += 1

    def send_b(origin, peer):
        nonlocal b_count
        pltpu.make_async_remote_copy(
            src_ref=packed(b_pack, origin),
            dst_ref=packed(b_pack, origin),
            send_sem=b_send.at[b_count],
            recv_sem=b_recv.at[origin],
            device_id={"col": peer},
        ).start()
        b_count += 1

    def wait_a(origin, s):
        tile = a_pack.at[SLOTS * origin + s]
        pltpu.make_async_copy(tile, tile, a_recv.at[SLOTS * origin + s]).wait()

    def wait_b(origin):
        arrived(b_pack, origin, b_recv.at[origin])

    sibling = col_of(zh, y, 1 - core)
    half = y_size // 2

    def others(at, size):
        return [k + 1 - (at - k + size - 1) // size for k in range(size - 1)]

    def around_x(origin, s):
        for to in others(x, x_size):
            send_a(origin, s, row_of(zl, to))

    far_count = 0

    def send_far(origin, s, d):
        nonlocal far_count
        tile = b_pack.at[SLOTS * origin + s]
        pltpu.make_async_remote_copy(
            src_ref=tile,
            dst_ref=tile,
            send_sem=far_send.at[far_count],
            recv_sem=far_recv.at[far_count],
            device_id={"col": y_at(zh, d)},
        ).start()
        far_count += 1

    def raw_arrival(n):
        origin = raw_origins[n]
        pltpu.make_async_copy(raw_in.at[n], raw_in.at[n], raw_recv.at[n]).wait()
        for s in range(SLOTS):
            stoch = (raw_in[n, s] / in_total[raw_cols[n][s]]).astype(jnp.bfloat16)
            b_pack[SLOTS * origin + s] = stoch

    def spread(zh_, d):
        sign = -1 if d > 0 else 1
        send_far(y_at(zh_, d), 0 if d > 0 else 1, 2 * sign)
        send_b(y_at(zh_, d), y_at(zh, sign))
        send_b(y_at(zh_, d), sibling)

    def arrive(zh_, d):
        wait_b(y_at(zh_, d))
        send_b(y_at(zh_, d), sibling)

    def z_arrival(zl_, s):
        origin = row_of(zl_, x)
        wait_a(origin, s)
        around_x(origin, s)

    for d in reach:
        if d not in raw_reach:
            send_b(c, y_at(zh, d))
    await_some(row_here, Z_LO - 1 - zl + x_size - 1 - x)
    for s in range(SLOTS):
        for to in others(zl, Z_LO):
            send_a(r, s, row_of(to, x))
    for s in range(SLOTS):
        around_x(r, s)
    send_b(c, sibling)
    raw_arrival(0)
    for d in reach:
        send_b(partner, y_at(zh, d))
    send_b(partner, sibling)
    for n, d in enumerate(raw_reach, 1):
        raw_arrival(n)
        spread(zh, d)
    for s in range(SLOTS):
        for zl_ in others(zl, Z_LO):
            z_arrival(zl_, s)
    for zh_ in (zh, other):
        for d in reach:
            if zh_ is zh and d in raw_reach:
                continue
            wait_b(y_at(zh_, d))
            if abs(d) == 2:
                spread(zh_, d)
            else:
                send_b(y_at(zh_, d), sibling)
    for zh_, d in ((zh, 3), (zh, -3), (other, 3), (other, -3)):
        arrive(zh_, d)
    for n, zh_ in ((0, zh), (2, other)):
        origin = y_at(zh_, half)
        for s in range(SLOTS):
            tile = b_pack.at[SLOTS * origin + s]
            pltpu.make_async_copy(tile, tile, far_recv.at[n + s]).wait()
        send_b(origin, sibling)

    for zl_ in range(Z_LO):
        for d in range(1, x_size):
            for s in range(SLOTS):
                wait_a(row_of((zl + zl_) % Z_LO, (x + d) % x_size), s)

    def wait_sibling(block, carry):
        wait_b(block * CORES + 1 - core)
        return carry

    lax.fori_loop(0, cols // CORES, wait_sibling, 0)

    result[...] = jnp.zeros_like(result)

    def multiply(block, carry):
        left, right = [], []
        for s in range(SLOTS):
            row_ = a_row[block * SLOTS + s]
            k = a_col[block * SLOTS + s]
            tile = a_pack[block * SLOTS + s]
            left.append(
                jnp.concatenate(
                    [jnp.where(row_ == i, tile, jnp.zeros_like(tile)) for i in range(tr)], axis=0
                )
            )
            right.append(jnp.concatenate([b_pack[b_slot[k + j]] for j in range(tc)], axis=1))
        result[...] += jnp.dot(
            jnp.concatenate(left, axis=1),
            jnp.concatenate(right, axis=0),
            preferred_element_type=jnp.float32,
        )
        return carry

    lax.fori_loop(0, rows, multiply, 0, unroll=16)

    sums = []
    for j in range(tc):
        col_sum = jnp.zeros((1, TILE), jnp.float32)
        for i in range(tr):
            at = (slice(i * TILE, (i + 1) * TILE), slice(j * TILE, (j + 1) * TILE))
            square = result[at]
            inflated = jnp.where(prune[i, j] > 0, square * square, 0.0)
            result[at] = inflated
            col_sum = col_sum + jnp.sum(inflated, axis=0, keepdims=True)
        sums.append(col_sum)
    out_own[...] = jnp.concatenate(sums, axis=1)

    exchange(all_peers, out_own, out_parts, out_send, out_recv)
    store = pltpu.make_async_copy(result, result_hbm, store_sem.at[0])
    store.start()

    @pl.when(zh == 0)
    def _():
        drain(pair_part, pair_sem.at[0])

    @pl.when(zh == 1)
    def _():
        drain(cross_parts, cross_send)

    for copy in raw_sends:
        copy.wait_send()
    drain(in_parts, in_send)
    for n in range(a_count):
        pltpu.make_async_copy(a_pack.at[0], a_pack.at[0], a_send.at[n]).wait()
    for n in range(b_count):
        arrived(b_pack, 0, b_send.at[n])
    for n in range(far_count):
        pltpu.make_async_copy(b_pack.at[0], b_pack.at[0], far_send.at[n]).wait()
    out_sum = collect(out_own, out_parts, out_recv)
    order = tr * TILE * cols
    scale[...] = order / out_sum
    store_scale = pltpu.make_async_copy(scale, scale_hbm, store_sem.at[1])
    store_scale.start()
    drain(out_parts, out_send)
    store.wait()
    store_scale.wait()


def on_device(rows, cols, values, pattern, prune):
    tr, tc = prune.shape
    height, width = values.shape
    f32, bf16 = jnp.float32, jnp.bfloat16
    dma = pltpu.SemaphoreType.DMA
    inflated, scale = pl.pallas_call(
        functools.partial(kernel, rows, cols),
        out_shape=[
            jax.ShapeDtypeStruct((height, width), f32),
            jax.ShapeDtypeStruct((1, width), f32),
        ],
        in_specs=[pl.BlockSpec(memory_space=pltpu.HBM)] * 3,
        out_specs=[pl.BlockSpec(memory_space=pl.ANY)] * 2,
        scratch_shapes=[
            pltpu.VMEM((tr * tc, TILE, TILE), f32),
            pltpu.SMEM(pattern.shape, jnp.int32),
            pltpu.SMEM(prune.shape, jnp.int32),
            pltpu.VMEM((SLOTS, TILE, TILE), f32),
            pltpu.VMEM((3, SLOTS, TILE, TILE), f32),
            pltpu.VMEM((1, 1, width), f32),
            pltpu.VMEM((cols // Z_HI, 1, width), f32),
            pltpu.VMEM((1, width), f32),
            pltpu.VMEM((1, width), f32),
            pltpu.VMEM((rows * SLOTS, TILE, TILE), bf16),
            pltpu.VMEM((cols * SLOTS + 1, TILE, TILE), bf16),
            pltpu.VMEM((1, width), f32),
            pltpu.VMEM((cols // Z_HI - 1, 1, width), f32),
            pltpu.VMEM((tc, 1, TILE), f32),
            pltpu.VMEM((1, width), f32),
            pltpu.VMEM((cols - 1, 1, width), f32),
            pltpu.VMEM((height, width), f32),
            pltpu.SMEM((cols * tr * tc,), jnp.int32),
            pltpu.SMEM((rows * SLOTS,), jnp.int32),
            pltpu.SMEM((rows * SLOTS,), jnp.int32),
            dma((tr * tc,)),
            dma((2,)),
            dma((2,)),
            dma((3,)),
            dma((3,)),
            dma((2,)),
            dma,
            dma,
            pltpu.SemaphoreType.REGULAR,
            pltpu.SemaphoreType.REGULAR,
            pltpu.SemaphoreType.REGULAR,
            dma((4,)),
            dma((4,)),
            dma,
            dma,
            dma,
            dma,
            dma((rows * SLOTS,)),
            dma((rows * SLOTS,)),
            dma((cols,)),
            dma((cols,)),
        ],
        compiler_params=pltpu.CompilerParams(
            collective_id=0,
            has_side_effects=True,
            vmem_limit_bytes=32 * 1024 * 1024,
        ),
        cost_estimate=pl.CostEstimate(
            flops=2 * height * width * TILE * SLOTS * rows,
            bytes_accessed=2 * 4 * height * width,
            transcendentals=0,
        ),
    )(*(pltpu.with_memory_space_constraint(x, pltpu.HBM) for x in (values, pattern, prune)))
    return inflated * scale


def solution(mesh):
    in_specs = (P("col", "row"), P(), P("col", "row"))
    out_specs = P("col", "row")
    return jax.shard_map(
        functools.partial(on_device, mesh.shape["row"], mesh.shape["col"]),
        mesh=mesh,
        in_specs=in_specs,
        out_specs=out_specs,
        check_vma=False,
    )
```

```python
import functools

import jax
import jax.numpy as jnp
from jax import lax
from jax.experimental import pallas as pl
from jax.experimental.pallas import tpu as pltpu
from jax.sharding import PartitionSpec as P

TILE = 128
SLOTS = 2
CORES = 2
Z_HI = 2
Z_LO = 4


def kernel(
    rows,
    cols,
    values_hbm,
    pattern_hbm,
    prune_hbm,
    result_hbm,
    scale_hbm,
    values,
    pattern,
    prune,
    raw_own,
    raw_in,
    pair_part,
    cross_parts,
    in_pair,
    scale,
    a_pack,
    b_pack,
    in_own,
    in_parts,
    in_total,
    out_own,
    out_parts,
    result,
    b_slot,
    a_row,
    a_col,
    load_sem,
    store_sem,
    fetch_sem,
    raw_send,
    raw_recv,
    pair_sem,
    cross_send,
    cross_recv,
    partner_here,
    half_here,
    row_here,
    far_send,
    far_recv,
    in_send,
    in_recv,
    out_send,
    out_recv,
    a_send,
    a_recv,
    b_send,
    b_recv,
):
    tr, tc = prune.shape
    x_size = rows // Z_LO
    y_size = cols // (CORES * Z_HI)
    r, c = lax.axis_index("row"), lax.axis_index("col")
    zl, x = r // x_size, r % x_size
    core = c % CORES
    y = (c // CORES) % y_size
    zh = c // (CORES * y_size)

    def row_of(zl_, x_):
        return zl_ * x_size + x_

    def col_of(zh_, y_, core_):
        return (zh_ * y_size + y_) * CORES + core_

    other = 1 - zh
    partner = col_of(other, y, core)

    def y_at(zh_, d):
        return col_of(zh_, (y + d + y_size) % y_size, core)

    def ring(d):
        return min(d, y_size - d)

    offsets = [(dz, dy, dc) for dz in range(Z_HI) for dy in range(y_size) for dc in range(CORES)]
    offsets.sort(key=lambda o: -(Z_LO * o[0] + ring(o[1])))
    offsets.remove((0, 0, 0))

    def at_offset(dz, dy, dc):
        return col_of((zh + dz) % Z_HI, (y + dy) % y_size, (core + dc) % CORES)

    half_peers = [at_offset(*o) for o in offsets if o[0] == 0]
    other_half = [at_offset(*o) for o in offsets if o[0] == 1]

    late_first = (rows - 1 - r) // (rows - 1) * (1 - zh)

    def rank_of(y_, core_):
        side = (y_ + y_size // 2 - 1) // y_size
        first = (y_size - 1 - y_) // (y_size - 1)
        place = ((1 - side) * (2 * y_ - 1) + side * 2 * (y_size - y_) + first) * CORES + core_
        return (place - late_first + cols // Z_HI) % (cols // Z_HI)

    rank = rank_of(y, core)
    half_ranks = [rank_of((y + dy) % y_size, (core + dc) % CORES) for dz, dy, dc in offsets if dz == 0]
    row_peers = [row_of((zl + d) % Z_LO, x) for d in (3, 2, 1)]
    row_peers += [row_of(zl, (x + d) % x_size) for d in range(1, x_size)]
    barrier = pltpu.get_barrier_semaphore()

    def await_some(sem, count):
        pl.when(count > 0)(lambda: pl.semaphore_wait(sem, count))

    def signal(sem, axis, peer):
        pl.semaphore_signal(sem, inc=1, device_id={axis: peer})

    @pl.when(zh == 0)
    def _():
        for peer in other_half:
            signal(barrier, "col", peer)

    for peer, peer_rank in zip(half_peers, half_ranks, strict=True):
        pl.when(peer_rank > rank)(functools.partial(signal, barrier, "col", peer))
    for peer in row_peers:
        pl.when(peer > r)(functools.partial(signal, barrier, "row", peer))
    await_some(barrier, rank + zl + x + zh * (cols // Z_HI))

    @pl.when(zh == 1)
    def _():
        signal(partner_here, "col", partner)

    for peer, peer_rank in zip(half_peers, half_ranks, strict=True):
        pl.when(peer_rank < rank)(functools.partial(signal, half_here, "col", peer))
    for peer in row_peers:
        pl.when(peer < r)(functools.partial(signal, row_here, "row", peer))

    loads = [
        pltpu.make_async_copy(
            values_hbm.at[pl.ds(t // tc * TILE, TILE), pl.ds(t % tc * TILE, TILE)],
            values.at[t],
            load_sem.at[t],
        )
        for t in range(tr * tc)
    ]
    fetches = [
        pltpu.make_async_copy(pattern_hbm, pattern, fetch_sem.at[0]),
        pltpu.make_async_copy(prune_hbm, prune, fetch_sem.at[1]),
    ]
    for copy in fetches + loads:
        copy.start()

    for copy in fetches:
        copy.wait()

    result[...] = jnp.zeros_like(result)

    def locate(block_row, block_col):
        seen = jnp.int32(0)
        place = [jnp.int32(0)] * SLOTS
        place_col = [jnp.int32(0)] * SLOTS
        for t in range(tr * tc):
            here = pattern[tr * block_row + t // tc, tc * block_col + t % tc]
            for s in range(SLOTS):
                hit = (here > 0) & (seen == s)
                place[s] = jnp.where(hit, t, place[s])
                place_col[s] = jnp.where(hit, t % tc, place_col[s])
            seen = seen + here
        return seen, place, place_col

    seen, place, place_col = locate(c, r)
    for copy in loads:
        copy.wait()
    tiles = []
    partial = [jnp.zeros((1, TILE), jnp.float32) for _ in range(tc)]
    for s in range(SLOTS):
        tile = jnp.where(seen > s, values[place[s]], 0.0)
        tiles.append(tile)
        raw_own[s] = tile
        total = jnp.sum(tile, axis=0, keepdims=True)
        for j in range(tc):
            partial[j] = partial[j] + jnp.where(place_col[s] == j, total, 0.0)
    in_own[...] = jnp.concatenate(partial, axis=1)

    def exchange(peers, own_ref, parts_ref, send_sem, recv_sem):
        for n, peer in enumerate(peers):
            pltpu.make_async_remote_copy(
                src_ref=own_ref,
                dst_ref=parts_ref.at[n],
                send_sem=send_sem,
                recv_sem=recv_sem,
                device_id={"col": peer},
            ).start()

    def collect(own_ref, parts_ref, recv_sem):
        pltpu.make_async_copy(parts_ref, parts_ref, recv_sem).wait()
        return own_ref[...] + jnp.sum(parts_ref[...], axis=0)

    def drain(parts_ref, send_sem):
        pltpu.make_async_copy(parts_ref, parts_ref, send_sem).wait()

    reach = (2, -2, 1, -1)
    raw_reach = (2, -2)
    raw_origins = [partner, *(y_at(zh, d) for d in raw_reach)]

    def raw_copy(peer, slot):
        return pltpu.make_async_remote_copy(
            src_ref=raw_own,
            dst_ref=raw_in.at[slot],
            send_sem=raw_send.at[slot],
            recv_sem=raw_recv.at[slot],
            device_id={"col": peer},
        )

    raw_sends = [raw_copy(partner, 0)]
    raw_sends += [raw_copy(y_at(zh, d), 1 + raw_reach.index(-d)) for d in raw_reach]

    @pl.when(zh == 1)
    def _():
        exchange(other_half, in_own, cross_parts, cross_send, cross_recv)
        raw_sends[0].start()

    await_some(half_here, cols // Z_HI - 1 - rank)
    exchange(half_peers, in_own, in_parts, in_send, in_recv)
    for copy in raw_sends[1:]:
        copy.start()

    def locate_b(block, carry):
        count = jnp.int32(0)
        for t in range(tr * tc):
            here = pattern[tr * block + t // tc, tc * r + t % tc]
            b_slot[block * tr * tc + t] = jnp.where(here > 0, SLOTS * block + count, SLOTS * cols)
            count = count + here
        return carry

    def locate_a(block, carry):
        count = jnp.int32(0)
        row_ = [jnp.int32(tr)] * SLOTS
        col_ = [jnp.int32(0)] * SLOTS
        for t in range(tr * tc):
            here = pattern[tr * c + t // tc, tc * block + t % tc]
            for s in range(SLOTS):
                hit = (here > 0) & (count == s)
                row_[s] = jnp.where(hit, t // tc, row_[s])
                col_[s] = jnp.where(hit, t % tc, col_[s])
            count = count + here
        for s in range(SLOTS):
            a_row[block * SLOTS + s] = row_[s]
            a_col[block * SLOTS + s] = tc * (tc * block + col_[s])
        return carry

    def locate_all():
        lax.fori_loop(0, cols, locate_b, 0)
        lax.fori_loop(0, rows, locate_a, 0)

    raw_cols = [locate(origin, r)[2] for origin in raw_origins]
    pl.when(zh == 1)(locate_all)
    in_pair[...] = collect(in_own, in_parts, in_recv)

    @pl.when(zh == 0)
    def _():
        pl.semaphore_wait(partner_here, 1)
        exchange([partner], in_pair, pair_part, pair_sem.at[0], pair_sem.at[1])
        raw_sends[0].start()

    def set_total(total):
        for j in range(tc):
            in_total[j] = total[:, j * TILE : (j + 1) * TILE]

    @pl.when(zh == 0)
    def _():
        locate_all()
        set_total(collect(in_pair, cross_parts, cross_recv))

    @pl.when(zh == 1)
    def _():
        set_total(collect(in_pair, pair_part, pair_sem.at[1]))

    for s in range(SLOTS):
        stoch = (tiles[s] / in_total[place_col[s]]).astype(jnp.bfloat16)
        a_pack[SLOTS * r + s] = stoch
        b_pack[SLOTS * c + s] = stoch
    b_pack[SLOTS * cols] = jnp.zeros((TILE, TILE), jnp.bfloat16)

    a_count, b_count = 0, 0

    def packed(ref, origin):
        return ref.at[pl.ds(SLOTS * origin, SLOTS)]

    def arrived(ref, origin, sem):
        pltpu.make_async_copy(packed(ref, origin), packed(ref, origin), sem).wait()

    def send_a(origin, s, peer):
        nonlocal a_count
        pltpu.make_async_remote_copy(
            src_ref=a_pack.at[SLOTS * origin + s],
            dst_ref=a_pack.at[SLOTS * origin + s],
            send_sem=a_send.at[a_count],
            recv_sem=a_recv.at[SLOTS * origin + s],
            device_id={"row": peer},
        ).start()
        a_count += 1

    def send_b(origin, peer):
        nonlocal b_count
        pltpu.make_async_remote_copy(
            src_ref=packed(b_pack, origin),
            dst_ref=packed(b_pack, origin),
            send_sem=b_send.at[b_count],
            recv_sem=b_recv.at[origin],
            device_id={"col": peer},
        ).start()
        b_count += 1

    def wait_a(origin, s):
        tile = a_pack.at[SLOTS * origin + s]
        pltpu.make_async_copy(tile, tile, a_recv.at[SLOTS * origin + s]).wait()

    def wait_b(origin):
        arrived(b_pack, origin, b_recv.at[origin])

    sibling = col_of(zh, y, 1 - core)
    half = y_size // 2

    def others(at, size):
        return [k + 1 - (at - k + size - 1) // size for k in range(size - 1)]

    def around_x(origin, s):
        for to in others(x, x_size):
            send_a(origin, s, row_of(zl, to))

    far_count = 0

    def send_far(origin, s, d):
        nonlocal far_count
        tile = b_pack.at[SLOTS * origin + s]
        pltpu.make_async_remote_copy(
            src_ref=tile,
            dst_ref=tile,
            send_sem=far_send.at[far_count],
            recv_sem=far_recv.at[far_count],
            device_id={"col": y_at(zh, d)},
        ).start()
        far_count += 1

    def raw_arrival(n):
        origin = raw_origins[n]
        pltpu.make_async_copy(raw_in.at[n], raw_in.at[n], raw_recv.at[n]).wait()
        for s in range(SLOTS):
            stoch = (raw_in[n, s] / in_total[raw_cols[n][s]]).astype(jnp.bfloat16)
            b_pack[SLOTS * origin + s] = stoch

    def spread(zh_, d):
        sign = -1 if d > 0 else 1
        send_far(y_at(zh_, d), 0 if d > 0 else 1, 2 * sign)
        send_b(y_at(zh_, d), y_at(zh, sign))
        send_b(y_at(zh_, d), sibling)

    def arrive(zh_, d):
        wait_b(y_at(zh_, d))
        send_b(y_at(zh_, d), sibling)

    def z_arrival(zl_, s):
        origin = row_of(zl_, x)
        wait_a(origin, s)
        around_x(origin, s)

    for d in reach:
        if d not in raw_reach:
            send_b(c, y_at(zh, d))
    await_some(row_here, Z_LO - 1 - zl + x_size - 1 - x)
    for s in range(SLOTS):
        for to in others(zl, Z_LO):
            send_a(r, s, row_of(to, x))
    for s in range(SLOTS):
        around_x(r, s)
    send_b(c, sibling)
    raw_arrival(0)
    for d in reach:
        send_b(partner, y_at(zh, d))
    send_b(partner, sibling)
    for n, d in enumerate(raw_reach, 1):
        raw_arrival(n)
        spread(zh, d)
    for s in range(SLOTS):
        for zl_ in others(zl, Z_LO)[:-1]:
            z_arrival(zl_, s)
    for s in range(SLOTS):
        z_arrival(others(zl, Z_LO)[-1], s)
    for zh_ in (zh, other):
        for d in reach:
            if zh_ is zh and d in raw_reach:
                continue
            wait_b(y_at(zh_, d))
            if abs(d) == 2:
                spread(zh_, d)
            else:
                send_b(y_at(zh_, d), sibling)
    for zh_, d in ((zh, 3), (zh, -3), (other, 3), (other, -3)):
        arrive(zh_, d)
    for n, zh_ in ((0, zh), (2, other)):
        origin = y_at(zh_, half)
        for s in range(SLOTS):
            tile = b_pack.at[SLOTS * origin + s]
            pltpu.make_async_copy(tile, tile, far_recv.at[n + s]).wait()
        send_b(origin, sibling)

    def wait_sibling(block, carry):
        wait_b(block * CORES + 1 - core)
        return carry

    lax.fori_loop(0, cols // CORES, wait_sibling, 0)

    def multiply(line):
        left, right = [], []
        for n in range(x_size * SLOTS):
            slot = line * x_size * SLOTS + n
            row_ = a_row[slot]
            k = a_col[slot]
            tile = a_pack[slot]
            left.append(
                jnp.concatenate(
                    [jnp.where(row_ == i, tile, jnp.zeros_like(tile)) for i in range(tr)], axis=0
                )
            )
            right.append(jnp.concatenate([b_pack[b_slot[k + j]] for j in range(tc)], axis=1))
        result[...] += jnp.dot(
            jnp.concatenate(left, axis=1),
            jnp.concatenate(right, axis=0),
            preferred_element_type=jnp.float32,
        )

    for line in (zl, *others(zl, Z_LO)):
        for d in range(1, x_size):
            for s in range(SLOTS):
                wait_a(row_of(line, (x + d) % x_size), s)
        multiply(line)

    sums = []
    for j in range(tc):
        col_sum = jnp.zeros((1, TILE), jnp.float32)
        for i in range(tr):
            at = (slice(i * TILE, (i + 1) * TILE), slice(j * TILE, (j + 1) * TILE))
            square = result[at]
            inflated = jnp.where(prune[i, j] > 0, square * square, 0.0)
            result[at] = inflated
            col_sum = col_sum + jnp.sum(inflated, axis=0, keepdims=True)
        sums.append(col_sum)
    out_own[...] = jnp.concatenate(sums, axis=1)

    for k in range(cols - 1):
        below = (c - k + cols - 1) // cols
        pltpu.make_async_remote_copy(
            src_ref=out_own,
            dst_ref=out_parts.at[c - below],
            send_sem=out_send,
            recv_sem=out_recv,
            device_id={"col": k + 1 - below},
        ).start()
    store = pltpu.make_async_copy(result, result_hbm, store_sem.at[0])
    store.start()

    @pl.when(zh == 0)
    def _():
        drain(pair_part, pair_sem.at[0])

    @pl.when(zh == 1)
    def _():
        drain(cross_parts, cross_send)

    for copy in raw_sends:
        copy.wait_send()
    drain(in_parts, in_send)
    for n in range(a_count):
        pltpu.make_async_copy(a_pack.at[0], a_pack.at[0], a_send.at[n]).wait()
    for n in range(b_count):
        arrived(b_pack, 0, b_send.at[n])
    for n in range(far_count):
        pltpu.make_async_copy(b_pack.at[0], b_pack.at[0], far_send.at[n]).wait()
    out_sum = collect(out_own, out_parts, out_recv)
    order = tr * TILE * cols
    scale[...] = order / out_sum
    store_scale = pltpu.make_async_copy(scale, scale_hbm, store_sem.at[1])
    store_scale.start()
    drain(out_parts, out_send)
    store.wait()
    store_scale.wait()


def on_device(rows, cols, values, pattern, prune):
    tr, tc = prune.shape
    height, width = values.shape
    f32, bf16 = jnp.float32, jnp.bfloat16
    dma = pltpu.SemaphoreType.DMA
    inflated, scale = pl.pallas_call(
        functools.partial(kernel, rows, cols),
        out_shape=[
            jax.ShapeDtypeStruct((height, width), f32),
            jax.ShapeDtypeStruct((1, width), f32),
        ],
        in_specs=[pl.BlockSpec(memory_space=pltpu.HBM)] * 3,
        out_specs=[pl.BlockSpec(memory_space=pl.ANY)] * 2,
        scratch_shapes=[
            pltpu.VMEM((tr * tc, TILE, TILE), f32),
            pltpu.SMEM(pattern.shape, jnp.int32),
            pltpu.SMEM(prune.shape, jnp.int32),
            pltpu.VMEM((SLOTS, TILE, TILE), f32),
            pltpu.VMEM((3, SLOTS, TILE, TILE), f32),
            pltpu.VMEM((1, 1, width), f32),
            pltpu.VMEM((cols // Z_HI, 1, width), f32),
            pltpu.VMEM((1, width), f32),
            pltpu.VMEM((1, width), f32),
            pltpu.VMEM((rows * SLOTS, TILE, TILE), bf16),
            pltpu.VMEM((cols * SLOTS + 1, TILE, TILE), bf16),
            pltpu.VMEM((1, width), f32),
            pltpu.VMEM((cols // Z_HI - 1, 1, width), f32),
            pltpu.VMEM((tc, 1, TILE), f32),
            pltpu.VMEM((1, width), f32),
            pltpu.VMEM((cols - 1, 1, width), f32),
            pltpu.VMEM((height, width), f32),
            pltpu.SMEM((cols * tr * tc,), jnp.int32),
            pltpu.SMEM((rows * SLOTS,), jnp.int32),
            pltpu.SMEM((rows * SLOTS,), jnp.int32),
            dma((tr * tc,)),
            dma((2,)),
            dma((2,)),
            dma((3,)),
            dma((3,)),
            dma((2,)),
            dma,
            dma,
            pltpu.SemaphoreType.REGULAR,
            pltpu.SemaphoreType.REGULAR,
            pltpu.SemaphoreType.REGULAR,
            dma((4,)),
            dma((4,)),
            dma,
            dma,
            dma,
            dma,
            dma((rows * SLOTS,)),
            dma((rows * SLOTS,)),
            dma((cols,)),
            dma((cols,)),
        ],
        compiler_params=pltpu.CompilerParams(
            collective_id=0,
            has_side_effects=True,
            vmem_limit_bytes=32 * 1024 * 1024,
        ),
        cost_estimate=pl.CostEstimate(
            flops=2 * height * width * TILE * SLOTS * rows,
            bytes_accessed=2 * 4 * height * width,
            transcendentals=0,
        ),
    )(*(pltpu.with_memory_space_constraint(x, pltpu.HBM) for x in (values, pattern, prune)))
    return inflated * scale


def solution(mesh):
    in_specs = (P("col", "row"), P(), P("col", "row"))
    out_specs = P("col", "row")
    return jax.shard_map(
        functools.partial(on_device, mesh.shape["row"], mesh.shape["col"]),
        mesh=mesh,
        in_specs=in_specs,
        out_specs=out_specs,
        check_vma=False,
    )
```

```python
import functools

import jax
import jax.numpy as jnp
from jax import lax
from jax.experimental import pallas as pl
from jax.experimental.pallas import tpu as pltpu
from jax.sharding import PartitionSpec as P

TILE = 128
SLOTS = 2
CORES = 2
Z_HI = 2
Z_LO = 4


def kernel(
    rows,
    cols,
    values_hbm,
    pattern_hbm,
    prune_hbm,
    result_hbm,
    scale_hbm,
    values,
    pattern,
    prune,
    raw_own,
    raw_in,
    pair_part,
    cross_parts,
    in_pair,
    scale,
    a_pack,
    b_pack,
    in_own,
    in_parts,
    in_total,
    out_own,
    out_parts,
    result,
    b_slot,
    a_row,
    a_col,
    load_sem,
    store_sem,
    fetch_sem,
    raw_send,
    raw_recv,
    pair_sem,
    cross_send,
    cross_recv,
    partner_here,
    half_here,
    row_here,
    far_send,
    far_recv,
    in_send,
    in_recv,
    out_send,
    out_recv,
    a_send,
    a_recv,
    b_send,
    b_recv,
):
    tr, tc = prune.shape
    x_size = rows // Z_LO
    y_size = cols // (CORES * Z_HI)
    r, c = lax.axis_index("row"), lax.axis_index("col")
    zl, x = r // x_size, r % x_size
    core = c % CORES
    y = (c // CORES) % y_size
    zh = c // (CORES * y_size)

    def row_of(zl_, x_):
        return zl_ * x_size + x_

    def col_of(zh_, y_, core_):
        return (zh_ * y_size + y_) * CORES + core_

    other = 1 - zh
    partner = col_of(other, y, core)

    def y_at(zh_, d):
        return col_of(zh_, (y + d + y_size) % y_size, core)

    def ring(d):
        return min(d, y_size - d)

    offsets = [(dz, dy, dc) for dz in range(Z_HI) for dy in range(y_size) for dc in range(CORES)]
    offsets.sort(key=lambda o: -(Z_LO * o[0] + ring(o[1])))
    offsets.remove((0, 0, 0))

    def at_offset(dz, dy, dc):
        return col_of((zh + dz) % Z_HI, (y + dy) % y_size, (core + dc) % CORES)

    half_peers = [at_offset(*o) for o in offsets if o[0] == 0]
    other_half = [at_offset(*o) for o in offsets if o[0] == 1]

    late_first = (rows - 1 - r) // (rows - 1) * (1 - zh)

    def rank_of(y_, core_):
        side = (y_ + y_size // 2 - 1) // y_size
        first = (y_size - 1 - y_) // (y_size - 1)
        place = ((1 - side) * (2 * y_ - 1) + side * 2 * (y_size - y_) + first) * CORES + core_
        return (place - late_first + cols // Z_HI) % (cols // Z_HI)

    rank = rank_of(y, core)
    half_ranks = [rank_of((y + dy) % y_size, (core + dc) % CORES) for dz, dy, dc in offsets if dz == 0]
    row_peers = [row_of((zl + d) % Z_LO, x) for d in (3, 2, 1)]
    row_peers += [row_of(zl, (x + d) % x_size) for d in range(1, x_size)]
    barrier = pltpu.get_barrier_semaphore()

    def await_some(sem, count):
        pl.when(count > 0)(lambda: pl.semaphore_wait(sem, count))

    def signal(sem, axis, peer):
        pl.semaphore_signal(sem, inc=1, device_id={axis: peer})

    @pl.when(zh == 0)
    def _():
        for peer in other_half:
            signal(barrier, "col", peer)

    for peer, peer_rank in zip(half_peers, half_ranks, strict=True):
        pl.when(peer_rank > rank)(functools.partial(signal, barrier, "col", peer))
    for peer in row_peers:
        pl.when(peer > r)(functools.partial(signal, barrier, "row", peer))
    await_some(barrier, rank + zl + x + zh * (cols // Z_HI))

    @pl.when(zh == 1)
    def _():
        signal(partner_here, "col", partner)

    for peer, peer_rank in zip(half_peers, half_ranks, strict=True):
        pl.when(peer_rank < rank)(functools.partial(signal, half_here, "col", peer))
    for peer in row_peers:
        pl.when(peer < r)(functools.partial(signal, row_here, "row", peer))

    loads = [
        pltpu.make_async_copy(
            values_hbm.at[pl.ds(t // tc * TILE, TILE), pl.ds(t % tc * TILE, TILE)],
            values.at[t],
            load_sem.at[t],
        )
        for t in range(tr * tc)
    ]
    fetches = [
        pltpu.make_async_copy(pattern_hbm, pattern, fetch_sem.at[0]),
        pltpu.make_async_copy(prune_hbm, prune, fetch_sem.at[1]),
    ]
    for copy in fetches + loads:
        copy.start()

    for copy in fetches:
        copy.wait()

    result[...] = jnp.zeros_like(result)

    def locate(block_row, block_col):
        seen = jnp.int32(0)
        place = [jnp.int32(0)] * SLOTS
        place_col = [jnp.int32(0)] * SLOTS
        for t in range(tr * tc):
            here = pattern[tr * block_row + t // tc, tc * block_col + t % tc]
            for s in range(SLOTS):
                hit = (here > 0) & (seen == s)
                place[s] = jnp.where(hit, t, place[s])
                place_col[s] = jnp.where(hit, t % tc, place_col[s])
            seen = seen + here
        return seen, place, place_col

    seen, place, place_col = locate(c, r)
    for copy in loads:
        copy.wait()
    tiles = []
    partial = [jnp.zeros((1, TILE), jnp.float32) for _ in range(tc)]
    for s in range(SLOTS):
        tile = jnp.where(seen > s, values[place[s]], 0.0)
        tiles.append(tile)
        raw_own[s] = tile
        total = jnp.sum(tile, axis=0, keepdims=True)
        for j in range(tc):
            partial[j] = partial[j] + jnp.where(place_col[s] == j, total, 0.0)
    in_own[...] = jnp.concatenate(partial, axis=1)

    def exchange(peers, own_ref, parts_ref, send_sem, recv_sem):
        for n, peer in enumerate(peers):
            pltpu.make_async_remote_copy(
                src_ref=own_ref,
                dst_ref=parts_ref.at[n],
                send_sem=send_sem,
                recv_sem=recv_sem,
                device_id={"col": peer},
            ).start()

    def collect(own_ref, parts_ref, recv_sem):
        pltpu.make_async_copy(parts_ref, parts_ref, recv_sem).wait()
        return own_ref[...] + jnp.sum(parts_ref[...], axis=0)

    def drain(parts_ref, send_sem):
        pltpu.make_async_copy(parts_ref, parts_ref, send_sem).wait()

    reach = (2, -2, 1, -1)
    raw_reach = (2, -2)
    raw_origins = [partner, *(y_at(zh, d) for d in raw_reach)]

    def raw_copy(peer, slot):
        return pltpu.make_async_remote_copy(
            src_ref=raw_own,
            dst_ref=raw_in.at[slot],
            send_sem=raw_send.at[slot],
            recv_sem=raw_recv.at[slot],
            device_id={"col": peer},
        )

    raw_sends = [raw_copy(partner, 0)]
    raw_sends += [raw_copy(y_at(zh, d), 1 + raw_reach.index(-d)) for d in raw_reach]

    @pl.when(zh == 1)
    def _():
        exchange(other_half, in_own, cross_parts, cross_send, cross_recv)
        raw_sends[0].start()

    await_some(half_here, cols // Z_HI - 1 - rank)
    exchange(half_peers, in_own, in_parts, in_send, in_recv)
    for copy in raw_sends[1:]:
        copy.start()

    def locate_b(block, carry):
        count = jnp.int32(0)
        for t in range(tr * tc):
            here = pattern[tr * block + t // tc, tc * r + t % tc]
            b_slot[block * tr * tc + t] = jnp.where(here > 0, SLOTS * block + count, SLOTS * cols)
            count = count + here
        return carry

    def locate_a(block, carry):
        count = jnp.int32(0)
        row_ = [jnp.int32(tr)] * SLOTS
        col_ = [jnp.int32(0)] * SLOTS
        for t in range(tr * tc):
            here = pattern[tr * c + t // tc, tc * block + t % tc]
            for s in range(SLOTS):
                hit = (here > 0) & (count == s)
                row_[s] = jnp.where(hit, t // tc, row_[s])
                col_[s] = jnp.where(hit, t % tc, col_[s])
            count = count + here
        for s in range(SLOTS):
            a_row[block * SLOTS + s] = row_[s]
            a_col[block * SLOTS + s] = tc * (tc * block + col_[s])
        return carry

    def locate_all():
        lax.fori_loop(0, cols, locate_b, 0)
        lax.fori_loop(0, rows, locate_a, 0)

    raw_cols = [locate(origin, r)[2] for origin in raw_origins]
    pl.when(zh == 1)(locate_all)
    in_pair[...] = collect(in_own, in_parts, in_recv)

    @pl.when(zh == 0)
    def _():
        pl.semaphore_wait(partner_here, 1)
        exchange([partner], in_pair, pair_part, pair_sem.at[0], pair_sem.at[1])
        raw_sends[0].start()

    def set_total(total):
        for j in range(tc):
            in_total[j] = total[:, j * TILE : (j + 1) * TILE]

    @pl.when(zh == 0)
    def _():
        locate_all()
        set_total(collect(in_pair, cross_parts, cross_recv))

    @pl.when(zh == 1)
    def _():
        set_total(collect(in_pair, pair_part, pair_sem.at[1]))

    for s in range(SLOTS):
        stoch = (tiles[s] / in_total[place_col[s]]).astype(jnp.bfloat16)
        a_pack[SLOTS * r + s] = stoch
        b_pack[SLOTS * c + s] = stoch
    b_pack[SLOTS * cols] = jnp.zeros((TILE, TILE), jnp.bfloat16)

    a_count, b_count = 0, 0

    def packed(ref, origin):
        return ref.at[pl.ds(SLOTS * origin, SLOTS)]

    def arrived(ref, origin, sem):
        pltpu.make_async_copy(packed(ref, origin), packed(ref, origin), sem).wait()

    def send_a(origin, s, peer):
        nonlocal a_count
        pltpu.make_async_remote_copy(
            src_ref=a_pack.at[SLOTS * origin + s],
            dst_ref=a_pack.at[SLOTS * origin + s],
            send_sem=a_send.at[a_count],
            recv_sem=a_recv.at[SLOTS * origin + s],
            device_id={"row": peer},
        ).start()
        a_count += 1

    def send_b(origin, peer):
        nonlocal b_count
        pltpu.make_async_remote_copy(
            src_ref=packed(b_pack, origin),
            dst_ref=packed(b_pack, origin),
            send_sem=b_send.at[b_count],
            recv_sem=b_recv.at[origin],
            device_id={"col": peer},
        ).start()
        b_count += 1

    def wait_a(origin, s):
        tile = a_pack.at[SLOTS * origin + s]
        pltpu.make_async_copy(tile, tile, a_recv.at[SLOTS * origin + s]).wait()

    def wait_b(origin):
        arrived(b_pack, origin, b_recv.at[origin])

    sibling = col_of(zh, y, 1 - core)
    half = y_size // 2

    def others(at, size):
        return [k + 1 - (at - k + size - 1) // size for k in range(size - 1)]

    def around_x(origin, s):
        for to in others(x, x_size):
            send_a(origin, s, row_of(zl, to))

    far_count = 0

    def send_far(origin, s, d):
        nonlocal far_count
        tile = b_pack.at[SLOTS * origin + s]
        pltpu.make_async_remote_copy(
            src_ref=tile,
            dst_ref=tile,
            send_sem=far_send.at[far_count],
            recv_sem=far_recv.at[far_count],
            device_id={"col": y_at(zh, d)},
        ).start()
        far_count += 1

    def raw_arrival(n):
        origin = raw_origins[n]
        pltpu.make_async_copy(raw_in.at[n], raw_in.at[n], raw_recv.at[n]).wait()
        for s in range(SLOTS):
            stoch = (raw_in[n, s] / in_total[raw_cols[n][s]]).astype(jnp.bfloat16)
            b_pack[SLOTS * origin + s] = stoch

    def spread(zh_, d):
        sign = -1 if d > 0 else 1
        send_far(y_at(zh_, d), 0 if d > 0 else 1, 2 * sign)
        send_b(y_at(zh_, d), y_at(zh, sign))
        send_b(y_at(zh_, d), sibling)

    def arrive(zh_, d):
        wait_b(y_at(zh_, d))
        send_b(y_at(zh_, d), sibling)

    def z_arrival(zl_, s):
        origin = row_of(zl_, x)
        wait_a(origin, s)
        around_x(origin, s)

    for d in reach:
        if d not in raw_reach:
            send_b(c, y_at(zh, d))
    await_some(row_here, Z_LO - 1 - zl + x_size - 1 - x)
    for s in range(SLOTS):
        for to in others(zl, Z_LO):
            send_a(r, s, row_of(to, x))
    for s in range(SLOTS):
        around_x(r, s)
    send_b(c, sibling)
    raw_arrival(0)
    for d in reach:
        send_b(partner, y_at(zh, d))
    send_b(partner, sibling)
    for n, d in enumerate(raw_reach, 1):
        raw_arrival(n)
        spread(zh, d)
    for s in range(SLOTS):
        for zl_ in others(zl, Z_LO)[:-1]:
            z_arrival(zl_, s)
    for s in range(SLOTS):
        z_arrival(others(zl, Z_LO)[-1], s)
    for zh_ in (zh, other):
        for d in reach:
            if zh_ is zh and d in raw_reach:
                continue
            wait_b(y_at(zh_, d))
            if abs(d) == 2:
                spread(zh_, d)
            else:
                send_b(y_at(zh_, d), sibling)
    for zh_, d in ((zh, 3), (zh, -3), (other, 3), (other, -3)):
        arrive(zh_, d)
    for n, zh_ in ((0, zh), (2, other)):
        origin = y_at(zh_, half)
        for s in range(SLOTS):
            tile = b_pack.at[SLOTS * origin + s]
            pltpu.make_async_copy(tile, tile, far_recv.at[n + s]).wait()
        send_b(origin, sibling)

    def wait_sibling(block, carry):
        wait_b(block * CORES + 1 - core)
        return carry

    lax.fori_loop(0, cols // CORES, wait_sibling, 0)

    def multiply(block):
        left, right = [], []
        for n in range(SLOTS):
            slot = block * SLOTS + n
            row_ = a_row[slot]
            k = a_col[slot]
            tile = a_pack[slot]
            left.append(
                jnp.concatenate(
                    [jnp.where(row_ == i, tile, jnp.zeros_like(tile)) for i in range(tr)], axis=0
                )
            )
            right.append(jnp.concatenate([b_pack[b_slot[k + j]] for j in range(tc)], axis=1))
        result[...] += jnp.dot(
            jnp.concatenate(left, axis=1),
            jnp.concatenate(right, axis=0),
            preferred_element_type=jnp.float32,
        )

    for line in (zl, *others(zl, Z_LO)):
        for d in (0, 1, x_size - 1, *range(2, x_size - 1)):
            block = row_of(line, (x + d) % x_size)
            if d:
                for s in range(SLOTS):
                    wait_a(block, s)
            multiply(block)

    sums = []
    for j in range(tc):
        col_sum = jnp.zeros((1, TILE), jnp.float32)
        for i in range(tr):
            at = (slice(i * TILE, (i + 1) * TILE), slice(j * TILE, (j + 1) * TILE))
            square = result[at]
            inflated = jnp.where(prune[i, j] > 0, square * square, 0.0)
            result[at] = inflated
            col_sum = col_sum + jnp.sum(inflated, axis=0, keepdims=True)
        sums.append(col_sum)
    out_own[...] = jnp.concatenate(sums, axis=1)

    for k in range(cols - 1):
        below = (c - k + cols - 1) // cols
        pltpu.make_async_remote_copy(
            src_ref=out_own,
            dst_ref=out_parts.at[c - below],
            send_sem=out_send,
            recv_sem=out_recv,
            device_id={"col": k + 1 - below},
        ).start()
    store = pltpu.make_async_copy(result, result_hbm, store_sem.at[0])
    store.start()

    @pl.when(zh == 0)
    def _():
        drain(pair_part, pair_sem.at[0])

    @pl.when(zh == 1)
    def _():
        drain(cross_parts, cross_send)

    for copy in raw_sends:
        copy.wait_send()
    drain(in_parts, in_send)
    for n in range(a_count):
        pltpu.make_async_copy(a_pack.at[0], a_pack.at[0], a_send.at[n]).wait()
    for n in range(b_count):
        arrived(b_pack, 0, b_send.at[n])
    for n in range(far_count):
        pltpu.make_async_copy(b_pack.at[0], b_pack.at[0], far_send.at[n]).wait()
    out_sum = collect(out_own, out_parts, out_recv)
    order = tr * TILE * cols
    scale[...] = order / out_sum
    store_scale = pltpu.make_async_copy(scale, scale_hbm, store_sem.at[1])
    store_scale.start()
    drain(out_parts, out_send)
    store.wait()
    store_scale.wait()


def on_device(rows, cols, values, pattern, prune):
    tr, tc = prune.shape
    height, width = values.shape
    f32, bf16 = jnp.float32, jnp.bfloat16
    dma = pltpu.SemaphoreType.DMA
    inflated, scale = pl.pallas_call(
        functools.partial(kernel, rows, cols),
        out_shape=[
            jax.ShapeDtypeStruct((height, width), f32),
            jax.ShapeDtypeStruct((1, width), f32),
        ],
        in_specs=[pl.BlockSpec(memory_space=pltpu.HBM)] * 3,
        out_specs=[pl.BlockSpec(memory_space=pl.ANY)] * 2,
        scratch_shapes=[
            pltpu.VMEM((tr * tc, TILE, TILE), f32),
            pltpu.SMEM(pattern.shape, jnp.int32),
            pltpu.SMEM(prune.shape, jnp.int32),
            pltpu.VMEM((SLOTS, TILE, TILE), f32),
            pltpu.VMEM((3, SLOTS, TILE, TILE), f32),
            pltpu.VMEM((1, 1, width), f32),
            pltpu.VMEM((cols // Z_HI, 1, width), f32),
            pltpu.VMEM((1, width), f32),
            pltpu.VMEM((1, width), f32),
            pltpu.VMEM((rows * SLOTS, TILE, TILE), bf16),
            pltpu.VMEM((cols * SLOTS + 1, TILE, TILE), bf16),
            pltpu.VMEM((1, width), f32),
            pltpu.VMEM((cols // Z_HI - 1, 1, width), f32),
            pltpu.VMEM((tc, 1, TILE), f32),
            pltpu.VMEM((1, width), f32),
            pltpu.VMEM((cols - 1, 1, width), f32),
            pltpu.VMEM((height, width), f32),
            pltpu.SMEM((cols * tr * tc,), jnp.int32),
            pltpu.SMEM((rows * SLOTS,), jnp.int32),
            pltpu.SMEM((rows * SLOTS,), jnp.int32),
            dma((tr * tc,)),
            dma((2,)),
            dma((2,)),
            dma((3,)),
            dma((3,)),
            dma((2,)),
            dma,
            dma,
            pltpu.SemaphoreType.REGULAR,
            pltpu.SemaphoreType.REGULAR,
            pltpu.SemaphoreType.REGULAR,
            dma((4,)),
            dma((4,)),
            dma,
            dma,
            dma,
            dma,
            dma((rows * SLOTS,)),
            dma((rows * SLOTS,)),
            dma((cols,)),
            dma((cols,)),
        ],
        compiler_params=pltpu.CompilerParams(
            collective_id=0,
            has_side_effects=True,
            vmem_limit_bytes=32 * 1024 * 1024,
        ),
        cost_estimate=pl.CostEstimate(
            flops=2 * height * width * TILE * SLOTS * rows,
            bytes_accessed=2 * 4 * height * width,
            transcendentals=0,
        ),
    )(*(pltpu.with_memory_space_constraint(x, pltpu.HBM) for x in (values, pattern, prune)))
    return inflated * scale


def solution(mesh):
    in_specs = (P("col", "row"), P(), P("col", "row"))
    out_specs = P("col", "row")
    return jax.shard_map(
        functools.partial(on_device, mesh.shape["row"], mesh.shape["col"]),
        mesh=mesh,
        in_specs=in_specs,
        out_specs=out_specs,
        check_vma=False,
    )
```
